512 devices in a mesh: seq: 32 (over y, z_lo), dp: 16 (over z_hi, x, core).
Axes of the slice: x: 4, y: 4, z: 16 (z_hi: 2, z_lo: 8; z = z_hi * 8 + z_lo), core: 2. Of those that a mesh axis runs over, the one named last changes fastest.
Arguments:
- tokens: bfloat16 [16, 8192, 768], P('dp', 'seq'), may hold values from -6 to 6
- cotangent: bfloat16 [16, 8192, 768], P('dp', 'seq'), may hold values from -6 to 6
- conv_kernel: float32 [3, 3, 768], replicated, may hold values from -3 to 3
- point_weight: bfloat16 [3, 768, 768], replicated, may hold values from -0.21875 to 0.21875
Outputs:
- grad_tokens: bfloat16 [16, 8192, 768], P('dp', 'seq')
- grad_point: float32 [3, 768, 768], P(None, 'seq', 'dp')
- grad_kernel: float32 [3, 3, 768], replicated
The draws below stay inside these ranges and needn't reach their ends.
All inputs are finite; a program needn't handle non-finite values.
Results may differ from the reference program's by a relative error of at most 0.035.
Values may be sent and summed in bfloat16 or wider, within the bound.
A program may use at most 64 MiB of HBM per device.

```python
import math
import jax
import jax.numpy as jnp
from jax import lax

C = 768
L_DEV = 256
LAYERS = 3
STRIDE0 = 4
SEQS = 16
LENGTH = 8192
N_SEQ = 32


def raised(drawn, rng, source, target, parts, factor):
    def block_of(position):
        return (jnp.arange(drawn.shape[position]) // (drawn.shape[position] // parts)).reshape((-1,) + (1,) * (drawn.ndim - 1 - position))

    one_side = jax.random.permutation(rng, parts)[block_of(target)]
    far = (block_of(target) + parts // 2) % parts
    return jnp.where((block_of(source) == one_side) | (block_of(source) == far), factor * drawn, drawn)


def level_of(stream_key, extent, pieces, low, largest):
    factor_of = 1.0
    for dim, blocks in pieces:
        draws = jax.random.uniform(jax.random.fold_in(jax.random.fold_in(stream_key, 6), dim), (blocks,), jnp.float32, low / len(pieces), largest / len(pieces))
        factor_of = factor_of * jnp.repeat(jnp.exp(draws), extent[dim] // blocks).reshape((-1,) + (1,) * (len(extent) - 1 - dim))
    return factor_of


def gaussian(key, dims, scale, most, cuts=(), held_as=jnp.bfloat16):
    level = level_of(key, dims, cuts, -0.22, 0.18) if cuts else 1.0
    result = jax.random.normal(key, dims, jnp.float32) * scale * level
    return jnp.minimum(jnp.maximum(result, -most), most).astype(held_as)


def gaussian_with(own_key, shape, width, reach, shards, heavy, kind=jnp.bfloat16):
    values = width * jax.random.normal(own_key, shape, jnp.float32)
    if shards:
        values = values * level_of(own_key, shape, shards, -0.22, 0.18)
    return jnp.clip(raised(values, jax.random.fold_in(own_key, 3), *heavy), -reach, reach).astype(kind)


def setup_inputs(seed: int = 0) -> dict:
    arg_keys = jax.random.split(jax.random.key(seed), 5)
    tokens = gaussian(arg_keys[0], (SEQS, LENGTH, C), 1.0, 6.0, ((0, 16), (1, 32)))
    cotangent = gaussian_with(arg_keys[1], (SEQS, LENGTH, C), 1.0, 6.0, ((0, 16), (1, 32)), (1, 2, 32, 2.75))
    conv_kernel = gaussian(arg_keys[2], (LAYERS, 3, C), 0.6, 3.0, (), jnp.float32)
    point_weight = gaussian(arg_keys[3], (LAYERS, C, C), C ** -0.5, 0.21875)
    return {"tokens": tokens, "cotangent": cotangent, "conv_kernel": conv_kernel, "point_weight": point_weight}


EPSILON = 1e-06

def shifted(values, offset):
    length = values.shape[0]
    if abs(offset) >= length:
        return jnp.zeros_like(values)
    padding = jnp.zeros((abs(offset), values.shape[1]), values.dtype)
    if offset > 0:
        return jnp.concatenate([padding, values[:length - offset]], axis=0)
    return jnp.concatenate([values[-offset:], padding], axis=0)

def gelu_back(hidden, spread):
    return jax.vjp(jax.nn.gelu, hidden)[1](spread)[0]

def one_sequence(tokens, cotangent, conv_kernel, point_weight):
    stream = tokens
    stored = []
    for layer_index in range(LAYERS):
        offset_rows = L_DEV * STRIDE0 * 2 ** layer_index
        stream_wide = stream.astype(jnp.float32)
        inv_rms = lax.rsqrt(lax.optimization_barrier(jnp.mean(stream_wide * stream_wide, axis=-1, keepdims=True)) + EPSILON)
        normal = stream_wide * inv_rms
        normed_bf = normal.astype(jnp.bfloat16)
        from_below = shifted(normed_bf, offset_rows)
        from_above = shifted(normed_bf, -offset_rows)
        kernel_row = conv_kernel[layer_index]
        hidden = kernel_row[0] * from_below.astype(jnp.float32) + kernel_row[1] * normed_bf.astype(jnp.float32) + kernel_row[2] * from_above.astype(jnp.float32)
        active = jax.nn.gelu(hidden).astype(jnp.bfloat16)
        stream = (stream_wide + jnp.dot(active, point_weight[layer_index], preferred_element_type=jnp.float32)).astype(jnp.bfloat16)
        stored.append((inv_rms, normal, normed_bf, from_below, from_above, hidden, active))
    gradient = cotangent.astype(jnp.float32)
    point_parts = [None] * LAYERS
    kernel_parts = [None] * LAYERS
    for layer_index in reversed(range(LAYERS)):
        offset_rows = L_DEV * STRIDE0 * 2 ** layer_index
        inv_rms, normal, normed_bf, from_below, from_above, hidden, active = stored[layer_index]
        kernel_row = conv_kernel[layer_index]
        upstream = gradient.astype(jnp.bfloat16)
        slab_act = active.reshape(N_SEQ, L_DEV, C).astype(jnp.float32)
        slab_up = upstream.reshape(N_SEQ, L_DEV, C).astype(jnp.float32)
        partial_value = jnp.einsum('ntc,ntd->ncd', slab_act, slab_up)
        rounded = lax.optimization_barrier(partial_value.astype(jnp.bfloat16))
        point_parts[layer_index] = lax.optimization_barrier(jnp.sum(rounded.astype(jnp.float32), axis=0))
        spread = jnp.dot(upstream, point_weight[layer_index].T, preferred_element_type=jnp.float32)
        grad_hidden = gelu_back(hidden, spread).astype(jnp.bfloat16)
        grad_wide = grad_hidden.astype(jnp.float32)
        kernel_parts[layer_index] = jnp.stack([lax.optimization_barrier(jnp.sum(grad_wide * from_below.astype(jnp.float32), axis=0)), lax.optimization_barrier(jnp.sum(grad_wide * normed_bf.astype(jnp.float32), axis=0)), lax.optimization_barrier(jnp.sum(grad_wide * from_above.astype(jnp.float32), axis=0))])
        grad_normed = kernel_row[1] * grad_wide + kernel_row[0] * shifted(grad_wide, -offset_rows) + kernel_row[2] * shifted(grad_wide, offset_rows)
        gradient = gradient + inv_rms * (grad_normed - normal * lax.optimization_barrier(jnp.mean(grad_normed * normal, axis=-1, keepdims=True)))
    return (gradient.astype(jnp.bfloat16), jnp.stack(point_parts), jnp.stack(kernel_parts))

def reference(tokens, cotangent, conv_kernel, point_weight):

    def per_sequence(running, inputs_pair):
        grad_seq, point_term, kernel_term = one_sequence(inputs_pair[0], inputs_pair[1], conv_kernel, point_weight)
        return ((running[0] + point_term, running[1] + kernel_term), grad_seq)
    initial = (jnp.zeros((LAYERS, C, C), jnp.float32), jnp.zeros((LAYERS, 3, C), jnp.float32))
    (point_total, kernel_total), grad_tokens = lax.scan(per_sequence, initial, (tokens, cotangent))
    factor = 1.0 / math.sqrt(SEQS * LENGTH)
    return (grad_tokens, point_total * factor, kernel_total * factor)
```

```python
import functools
import math

import jax
import jax.numpy as jnp
from jax import lax
from jax.experimental import pallas as pl
from jax.experimental.pallas import tpu as pltpu

EPSILON = 1e-06
MESH = pl.DeviceIdType.MESH
F32 = jnp.float32
BF16 = jnp.bfloat16

C = 768
LAYERS = 3
CHAIN = 8
ROWS = 16
PARTS = 2
SLAB = 256
COLS = 256
GELU_A = math.sqrt(2.0 / math.pi)
GELU_B = 0.044715


def kernel(factor, tok, cot, taps, weight, out, out_point, out_taps, *scratch):
    (xin, normed, normal, inverse, slope, active, up, grad, grad_hid, ready, w, acc, terms, sibling, summed, from_x, turned,
     to_y, from_y, to_z, from_z, to_block, from_block, taps_acc, taps_out, taps_in,
     tok_send, tok_recv, cot_send, cot_recv, out_send, out_recv, own_sem, w_sem, red_send, red_recv) = scratch
    seq = lax.axis_index("seq")
    dp = lax.axis_index("dp")
    k, c = seq // 4, seq % 4
    y, h = seq // 8, (seq // 4) % 2
    zh, x, core = dp // 8, (dp // 2) % 4, dp % 2
    block = zh * 2 + h

    def chain_peer(i):
        j = (k + i) % CHAIN
        return j, (j * 4 + c, dp)

    def step_peer(stage, i):
        if stage == 0:
            return 1 - core, (seq, dp + 1 - 2 * core)
        if stage == 1:
            place = (x + i) % 4
            return place, (seq, zh * 8 + place * 2 + core)
        if stage == 2:
            place = (y + i) % 4
            return place, (place * 8 + h * 4 + c, dp)
        if stage == 3:
            place = (c + i) % 4
            return place, (seq - c + place, dp)
        place = (block + i) % 4
        return place, (y * 8 + (place % 2) * 4 + c, (place // 2) * 8 + dp % 8)

    barrier = pltpu.get_barrier_semaphore()

    def greet(peer):
        pl.semaphore_signal(barrier, inc=1, device_id=peer, device_id_type=MESH)

    @pl.loop(1, CHAIN)
    def _(i):
        greet(chain_peer(i)[1])

    greet(step_peer(0, 1)[1])

    @pl.loop(1, 4)
    def _(i):
        greet(step_peer(1, i)[1])
        greet(step_peer(3, i)[1])

    @pl.loop(0, 2)
    def _(i):
        greet((y * 8 + i * 4 + c, (1 - zh) * 8 + dp % 8))

    pl.semaphore_wait(barrier, 16)

    def rows_of(j, a):
        return pl.ds(pl.multiple_of(j * (PARTS * ROWS) + a * ROWS, ROWS), ROWS)

    def crossing_first(t):
        return 2 * t + 1 - 7 * (t // 4)

    def deal(src, dst_of, send, recv, a, i):
        j, peer = chain_peer(i)
        return pltpu.make_async_remote_copy(
            src_ref=src.at[rows_of(j, a)], dst_ref=dst_of(a, k), send_sem=send.at[a, i - 1], recv_sem=recv.at[a, i - 1],
            device_id=peer, device_id_type=MESH)

    def dealt(src, dst_of, send, recv, a, i):
        j = (k + CHAIN - i) % CHAIN
        return pltpu.make_async_remote_copy(
            src_ref=src.at[rows_of(j, a)], dst_ref=dst_of(a, j), send_sem=send.at[a, i - 1], recv_sem=recv.at[a, i - 1],
            device_id=chain_peer(i)[1], device_id_type=MESH)

    def tok_slot(a, j):
        return xin.at[a, j]

    def cot_slot(a, j):
        return up.at[LAYERS - 1, a, j]

    def own_tok(a):
        return pltpu.make_async_copy(tok.at[rows_of(k, a)], xin.at[a, k], own_sem.at[a])

    def own_cot(a):
        return pltpu.make_async_copy(cot.at[rows_of(k, a)], up.at[LAYERS - 1, a, k], own_sem.at[PARTS + a])

    def own_out(a):
        return pltpu.make_async_copy(ready.at[a, k], out.at[rows_of(k, a)], own_sem.at[2 * PARTS + a])

    def give_back(a, i):
        j, peer = chain_peer(i)
        return pltpu.make_async_remote_copy(
            src_ref=ready.at[a, j], dst_ref=out.at[rows_of(k, a)], send_sem=out_send.at[a, i - 1],
            recv_sem=out_recv.at[a, i - 1], device_id=peer, device_id_type=MESH)

    def given_back(a, i):
        j = (k + CHAIN - i) % CHAIN
        return pltpu.make_async_remote_copy(
            src_ref=ready.at[a, j], dst_ref=out.at[rows_of(j, a)], send_sem=out_send.at[a, i - 1],
            recv_sem=out_recv.at[a, i - 1], device_id=chain_peer(i)[1], device_id_type=MESH)

    for a in range(PARTS):
        @pl.loop(0, CHAIN - 1)
        def _(t):
            deal(tok, tok_slot, tok_send, tok_recv, a, crossing_first(t)).start()

        own_tok(a).start()
    for a in range(PARTS):
        @pl.loop(0, CHAIN - 1)
        def _(t):
            deal(cot, cot_slot, cot_send, cot_recv, a, crossing_first(t)).start()

        own_cot(a).start()
    for layer in range(LAYERS):
        pltpu.make_async_copy(weight.at[layer], w.at[layer], w_sem.at[layer]).start()

    zeros = jnp.zeros((4, ROWS, C), BF16)
    for layer in range(LAYERS):
        for a in range(PARTS):
            normed[layer, a, 0:4] = zeros
            normed[layer, a, 12:16] = zeros
    grad_hid[0:4] = zeros
    grad_hid[12:16] = zeros
    taps_acc[...] = jnp.zeros_like(taps_acc)
    taps_out[...] = jnp.zeros_like(taps_out)

    def forward(a):
        for layer in range(LAYERS):
            shift = 2**layer

            @pl.loop(0, CHAIN)
            def _(j):
                value = xin[a, j].astype(F32)
                mean = jnp.sum(value * value, axis=-1, keepdims=True) * (1.0 / C)
                inv = lax.rsqrt(mean + EPSILON)
                value = value * inv
                inverse[layer, a, j] = jnp.broadcast_to(inv, (ROWS, 128))
                normal[layer, a, j] = value
                normed[layer, a, 4 + j] = value.astype(BF16)

            @pl.loop(0, CHAIN)
            def _(j):
                hid = (
                    taps[layer, 0:1, :] * normed[layer, a, 4 + j - shift].astype(F32)
                    + taps[layer, 1:2, :] * normed[layer, a, 4 + j].astype(F32)
                    + taps[layer, 2:3, :] * normed[layer, a, 4 + j + shift].astype(F32)
                )
                square = hid * hid
                tanh = jnp.tanh(GELU_A * hid * (1.0 + GELU_B * square))
                half = 0.5 * (1.0 + tanh)
                active[layer, a, j] = (hid * half).astype(BF16)
                slope[layer, a, j] = half + (0.5 * GELU_A) * hid * (1.0 - tanh * tanh) * (1.0 + (3.0 * GELU_B) * square)

            if layer == LAYERS - 1:
                continue
            if a == 0:
                pltpu.make_async_copy(weight.at[layer], w.at[layer], w_sem.at[layer]).wait()
            for n in range(C // COLS):
                cols = slice(n * COLS, (n + 1) * COLS)
                product = jnp.dot(active[layer, a].reshape(CHAIN * ROWS, C), w[layer, :, cols], preferred_element_type=F32)
                xin[a, :, :, cols] = (
                    xin[a, :, :, cols].astype(F32) + product.reshape(CHAIN, ROWS, COLS)).astype(BF16)

    def backward(a, layer):
        shift = 2**layer
        if a == 0 and layer == LAYERS - 1:
            pltpu.make_async_copy(weight.at[layer], w.at[layer], w_sem.at[layer]).wait()
        for n in range(C // COLS):
            cols = slice(n * COLS, (n + 1) * COLS)
            spread = lax.dot_general(
                up[layer, a].reshape(CHAIN * ROWS, C), w[layer, cols, :], (((1,), (1,)), ((), ())),
                preferred_element_type=F32)
            grad_hid[4:12, :, cols] = (spread.reshape(CHAIN, ROWS, COLS) * slope[layer, a, :, :, cols]).astype(BF16)

        @pl.loop(0, CHAIN)
        def _(j):
            mid = grad_hid[4 + j].astype(F32)
            for t in range(3):
                term = mid * normed[layer, a, 4 + j + (t - 1) * shift].astype(F32)
                taps_acc[layer, t] += term[0:8] + term[8:16]
            moved = (
                taps[layer, 1:2, :] * mid
                + taps[layer, 0:1, :] * grad_hid[4 + j + shift].astype(F32)
                + taps[layer, 2:3, :] * grad_hid[4 + j - shift].astype(F32)
            )
            value = normal[layer, a, j]
            mean = jnp.sum(moved * value, axis=-1, keepdims=True) * (1.0 / C)
            before = up[layer, a, j].astype(F32) if layer == LAYERS - 1 else grad[j]
            after = before + inverse[layer, a, j, :, 0:1] * (moved - value * mean)
            if layer > 0:
                grad[j] = after
                up[layer - 1, a, j] = after.astype(BF16)
            else:
                ready[a, j] = after.astype(BF16)

    def parcel(layer, stage, i, mine):
        place, peer = step_peer(stage, i)
        if stage == 0:
            src, dst = terms.at[layer, place], sibling.at[layer]
        elif stage == 1:
            src, dst = summed.at[layer, :, place], from_x.at[layer, i - 1]
        elif stage == 2:
            src, dst = to_y.at[layer, place], from_y.at[layer, i - 1]
        elif stage == 3:
            src, dst = to_z.at[layer, place], from_z.at[layer, i - 1]
        else:
            src, dst = to_block.at[layer, place % 2], from_block.at[layer, i - 1]
        if mine:
            src, dst = taps_out.at[layer, stage], taps_in.at[layer, stage, i - 1]
        kind = 1 if mine else 0
        return pltpu.make_async_remote_copy(
            src_ref=src, dst_ref=dst, send_sem=red_send.at[layer, stage, i - 1, kind],
            recv_sem=red_recv.at[layer, stage, i - 1, kind], device_id=peer, device_id_type=MESH)

    def partners(stage):
        return range(1, 2 if stage == 0 else 4)

    def send(layer, stage):
        for i in partners(stage):
            parcel(layer, stage, i, False).start()
            parcel(layer, stage, i, True).start()

    def arrive(layer, stage):
        for i in partners(stage):
            parcel(layer, stage, i, False).wait_recv()
            parcel(layer, stage, i, True).wait_recv()
        total = taps_out[layer, stage]
        for i in partners(stage):
            total = total + taps_in[layer, stage, i - 1]
        taps_out[layer, stage + 1] = total

    def point_terms(layer):
        rows = up[layer].reshape(PARTS * CHAIN * ROWS, C)
        acts = active[layer].reshape(PARTS * CHAIN * ROWS, C)
        for m in range(2):
            part = rows[:, m * 384:(m + 1) * 384]
            for n in range(C // COLS):
                cols = slice(n * COLS, (n + 1) * COLS)
                product = lax.dot_general(
                    part, acts[:, cols], (((0,), (0,)), ((), ())), preferred_element_type=F32)
                product = product.astype(BF16).reshape(4, 2, 48, COLS)
                for owner in range(2):
                    terms[layer, owner, m * 4:(m + 1) * 4, :, cols] = product[:, owner]
        for t in range(3):
            line = jnp.sum(taps_acc[layer, t], axis=0, keepdims=True)
            for b in range(C // 128):
                taps_out[layer, 0, t, b:b + 1, :] = line[:, b * 128:(b + 1) * 128]

    def after_core(layer):
        @pl.loop(0, 8)
        def _(b):
            summed[layer, b // 4, b % 4] = (
                terms[layer, core, b].astype(F32) + sibling[layer, b].astype(F32)).astype(BF16)

    def after_x(layer):
        for b in range(C // 128):
            lanes = slice(b * 128, (b + 1) * 128)
            halves = []
            for half in range(2):
                total = summed[layer, half, x, :, lanes].astype(F32)
                for i in range(3):
                    total = total + from_x[layer, i, half, :, lanes].astype(F32)
                halves.append(total)
            halves.append(jnp.zeros((32, 128), F32))
            turned[lanes, :] = jnp.concatenate(halves, axis=0).T

        @pl.loop(0, 32)
        def _(g):
            value = turned[pl.ds(pl.multiple_of(g * 24, 8), 24), :]
            value = jnp.concatenate([value, jnp.zeros((8, 128), F32)], axis=0)
            to_y[layer, g // 8, g % 4, (g // 4) % 2] = value.astype(BF16)

    def after_y(layer):
        total = to_y[layer, y].astype(F32)
        for i in range(3):
            total = total + from_y[layer, i].astype(F32)
        to_z[layer] = total.astype(BF16)

    def after_z(layer):
        total = to_z[layer, c].astype(F32)
        for i in range(3):
            total = total + from_z[layer, i].astype(F32)
        to_block[layer] = total.astype(BF16)

    def after_block(layer):
        total = to_block[layer, h].astype(F32)
        for i in range(3):
            total = total + from_block[layer, i].astype(F32)
        upper = jnp.broadcast_to(zh, (24, 48)) > 0
        out_point[layer] = jnp.where(upper, total[0:24, 48:96], total[0:24, 0:48]) * factor
        sums = taps_out[layer, 5] * factor
        for t in range(3):
            for b in range(C // 128):
                out_taps[layer, t:t + 1, b * 128:(b + 1) * 128] = sums[t, b:b + 1, :]

    follow = (after_core, after_x, after_y, after_z, after_block)

    def advance(layer, stage):
        arrive(layer, stage)
        follow[stage](layer)
        if stage < 4:
            send(layer, stage + 1)

    def wait_dealt(src, slot, sends, recvs, own, a):
        @pl.loop(1, CHAIN)
        def _(i):
            dealt(src, slot, sends, recvs, a, i).wait_recv()

        own(a).wait()

    def send_back(a):
        @pl.loop(0, CHAIN - 1)
        def _(t):
            give_back(a, crossing_first(t)).start()

        own_out(a).start()

    for a in range(PARTS):
        wait_dealt(tok, tok_slot, tok_send, tok_recv, own_tok, a)
        forward(a)
    wait_dealt(cot, cot_slot, cot_send, cot_recv, own_cot, 0)
    for layer in (2, 1, 0):
        backward(0, layer)
    send_back(0)
    wait_dealt(cot, cot_slot, cot_send, cot_recv, own_cot, 1)
    backward(1, 2)
    point_terms(2)
    send(2, 0)
    backward(1, 1)
    point_terms(1)
    send(1, 0)
    advance(2, 0)
    backward(1, 0)
    send_back(1)
    point_terms(0)
    send(0, 0)
    advance(1, 0)
    advance(2, 1)
    advance(0, 0)
    advance(2, 2)
    advance(1, 1)
    advance(2, 3)
    advance(1, 2)
    advance(0, 1)
    advance(2, 4)
    advance(1, 3)
    advance(0, 2)
    advance(1, 4)
    advance(0, 3)
    advance(0, 4)

    for a in range(PARTS):
        own_out(a).wait()

        @pl.loop(1, CHAIN)
        def _(i):
            given_back(a, i).wait_recv()
            give_back(a, i).wait_send()
            deal(tok, tok_slot, tok_send, tok_recv, a, i).wait_send()
            deal(cot, cot_slot, cot_send, cot_recv, a, i).wait_send()
    for layer in range(LAYERS):
        for stage in range(5):
            for i in partners(stage):
                parcel(layer, stage, i, False).wait_send()
                parcel(layer, stage, i, True).wait_send()


def local(factor, tokens, cotangent, conv_kernel, point_weight):
    any_space = pl.BlockSpec(memory_space=pl.ANY)
    vmem = pl.BlockSpec(memory_space=pltpu.VMEM)
    part = (PARTS, CHAIN, ROWS, C)
    scratch = [
        pltpu.VMEM(part, BF16),
        pltpu.VMEM((LAYERS, PARTS, CHAIN + 8, ROWS, C), BF16),
        pltpu.VMEM((LAYERS,) + part, F32),
        pltpu.VMEM((LAYERS, PARTS, CHAIN, ROWS, 128), F32),
        pltpu.VMEM((LAYERS,) + part, F32),
        pltpu.VMEM((LAYERS,) + part, BF16),
        pltpu.VMEM((LAYERS,) + part, BF16),
        pltpu.VMEM((CHAIN, ROWS, C), F32),
        pltpu.VMEM((CHAIN + 8, ROWS, C), BF16),
        pltpu.VMEM(part, BF16),
        pltpu.VMEM((LAYERS, C, C), BF16),
        pltpu.VMEM((8, 128), F32),
        pltpu.VMEM((LAYERS, 2, 8, 48, C), BF16),
        pltpu.VMEM((LAYERS, 8, 48, C), BF16),
        pltpu.VMEM((LAYERS, 2, 4, 48, C), BF16),
        pltpu.VMEM((LAYERS, 3, 2, 48, C), BF16),
        pltpu.VMEM((C, 128), F32),
        pltpu.VMEM((LAYERS, 4, 4, 2, 32, 128), BF16),
        pltpu.VMEM((LAYERS, 3, 4, 2, 32, 128), BF16),
        pltpu.VMEM((LAYERS, 4, 2, 32, 128), BF16),
        pltpu.VMEM((LAYERS, 3, 2, 32, 128), BF16),
        pltpu.VMEM((LAYERS, 2, 32, 128), BF16),
        pltpu.VMEM((LAYERS, 3, 32, 128), BF16),
        pltpu.VMEM((LAYERS, 3, 8, C), F32),
        pltpu.VMEM((LAYERS, 6, 3, 8, 128), F32),
        pltpu.VMEM((LAYERS, 5, 3, 3, 8, 128), F32),
        pltpu.SemaphoreType.DMA((PARTS, CHAIN - 1)),
        pltpu.SemaphoreType.DMA((PARTS, CHAIN - 1)),
        pltpu.SemaphoreType.DMA((PARTS, CHAIN - 1)),
        pltpu.SemaphoreType.DMA((PARTS, CHAIN - 1)),
        pltpu.SemaphoreType.DMA((PARTS, CHAIN - 1)),
        pltpu.SemaphoreType.DMA((PARTS, CHAIN - 1)),
        pltpu.SemaphoreType.DMA((3 * PARTS,)),
        pltpu.SemaphoreType.DMA((LAYERS,)),
        pltpu.SemaphoreType.DMA((LAYERS, 5, 3, 2)),
        pltpu.SemaphoreType.DMA((LAYERS, 5, 3, 2)),
    ]
    out, out_point, out_taps = pl.pallas_call(
        functools.partial(kernel, factor),
        out_shape=(
            jax.ShapeDtypeStruct((SLAB, C), BF16),
            jax.ShapeDtypeStruct((LAYERS, 24, 48), F32),
            jax.ShapeDtypeStruct((LAYERS, 3, C), F32),
        ),
        in_specs=[any_space, any_space, vmem, any_space],
        out_specs=(any_space, vmem, vmem),
        scratch_shapes=scratch,
        compiler_params=pltpu.CompilerParams(collective_id=0, has_side_effects=True, vmem_limit_bytes=48 * 2**20),
        cost_estimate=pl.CostEstimate(flops=2 * 9 * SLAB * C * C, bytes_accessed=6 * 2**20, transcendentals=LAYERS * SLAB * C),
    )(tokens[0], cotangent[0], conv_kernel, point_weight)
    return out[None], out_point, out_taps


def solution(mesh):
    factor = 1.0 / math.sqrt(mesh.shape["seq"] * mesh.shape["dp"] * SLAB)
    P = jax.sharding.PartitionSpec
    return jax.shard_map(
        functools.partial(local, factor),
        mesh=mesh,
        in_specs=(P("dp", "seq", None), P("dp", "seq", None), P(), P()),
        out_specs=(P("dp", "seq", None), P(None, "seq", "dp"), P()),
        check_vma=False,
    )
```

```python
import functools
import math

import jax
import jax.numpy as jnp
from jax import lax
from jax.experimental import pallas as pl
from jax.experimental.pallas import tpu as pltpu

EPSILON = 1e-06
MESH = pl.DeviceIdType.MESH
F32 = jnp.float32
BF16 = jnp.bfloat16

C = 768
LAYERS = 3
CHAIN = 8
ROWS = 16
PARTS = 2
SLAB = 256
COLS = 256
HALF = C // 2
PIECE = 96
GELU_A = math.sqrt(2.0 / math.pi)
GELU_B = 0.044715


def kernel(factor, tok, cot, taps_hbm, weight, out, out_point, out_taps, *scratch):
    (xin, normed, normal, inverse, slope, active, up, grad, grad_hid, ready, w, taps, terms, sibling, summed, half_way, from_a,
     turned, to_b, from_b, to_z, from_z, to_block, from_block, taps_acc, taps_part, taps_one, taps_in, taps_all,
     tok_send, tok_recv, cot_send, cot_recv, out_send, out_recv, own_sem, w_sem, core_sem, a_send, a_recv, red_send, red_recv,
     last_send, last_recv, tap_send, tap_recv) = scratch
    seq = lax.axis_index("seq")
    dp = lax.axis_index("dp")
    k, c = seq // 4, seq % 4
    y, h = seq // 8, (seq // 4) % 2
    zh, x, core = dp // 8, (dp // 2) % 4, dp % 2
    block = zh * 2 + h
    p = x + core * (y - x)
    r = y + core * (x - y)

    def chain_peer(i):
        j = (k + i) % CHAIN
        return j, (j * 4 + c, dp)

    def first_peer(place):
        return seq + core * (place - y) * 8, dp + (1 - core) * (place - x) * 2

    def step_peer(step, i):
        if step == 0:
            place = (r + i) % 4
            return place, (seq + (1 - core) * (place - y) * 8, dp + core * (place - x) * 2)
        place = (c + i) % 4
        return place, (seq - c + place, dp)

    def owner(e):
        return y * 8 + (e // 2) * 4 + c, core * 8 + x * 2 + e % 2

    def tap_peer(step, i):
        if step in (0, 4):
            place = (dp % 8 + i) % 8
            return place, (seq, zh * 8 + place)
        if step == 1:
            place = (y + i) % 4
            return place, (place * 8 + h * 4 + c, dp)
        if step == 2:
            return step_peer(1, i)
        place = (block + i) % 4
        return place, (y * 8 + (place % 2) * 4 + c, (place // 2) * 8 + dp % 8)

    barrier = pltpu.get_barrier_semaphore()

    def greet(peer):
        pl.semaphore_signal(barrier, inc=1, device_id=peer, device_id_type=MESH)

    @pl.loop(1, CHAIN)
    def _(i):
        greet(chain_peer(i)[1])
        greet(tap_peer(0, i)[1])

    @pl.loop(1, 4)
    def _(i):
        greet(step_peer(1, i)[1])

    @pl.loop(0, 4)
    def _(i):
        greet((y * 8 + (i // 2) * 4 + c, (1 - zh) * 8 + x * 2 + i % 2))

    greet((y * 8 + (1 - h) * 4 + c, zh * 8 + x * 2 + 1 - core))

    def load(layer):
        return pltpu.make_async_copy(weight.at[layer], w.at[layer], w_sem.at[layer])

    load_taps = pltpu.make_async_copy(taps_hbm, taps, w_sem.at[LAYERS])
    load_taps.start()
    for layer in range(LAYERS):
        load(layer).start()

    pl.semaphore_wait(barrier, 22)

    def rows_of(j, a):
        return pl.ds(pl.multiple_of(j * (PARTS * ROWS) + a * ROWS, ROWS), ROWS)

    def crossing_first(t):
        return 2 * t + 1 - 7 * (t // 4)

    def deal(src, dst_of, send, recv, a, i):
        j, peer = chain_peer(i)
        return pltpu.make_async_remote_copy(
            src_ref=src.at[rows_of(j, a)], dst_ref=dst_of(a, k), send_sem=send.at[a, i - 1], recv_sem=recv.at[a, i - 1],
            device_id=peer, device_id_type=MESH)

    def dealt(src, dst_of, send, recv, a, i):
        j = (k + CHAIN - i) % CHAIN
        return pltpu.make_async_remote_copy(
            src_ref=src.at[rows_of(j, a)], dst_ref=dst_of(a, j), send_sem=send.at[a, i - 1], recv_sem=recv.at[a, i - 1],
            device_id=chain_peer(i)[1], device_id_type=MESH)

    def tok_slot(a, j):
        return xin.at[a, j]

    def cot_slot(a, j):
        return up.at[LAYERS - 1, a, j]

    def own_tok(a):
        return pltpu.make_async_copy(tok.at[rows_of(k, a)], xin.at[a, k], own_sem.at[a])

    def own_cot(a):
        return pltpu.make_async_copy(cot.at[rows_of(k, a)], up.at[LAYERS - 1, a, k], own_sem.at[PARTS + a])

    def own_out(a):
        return pltpu.make_async_copy(ready.at[a, k], out.at[rows_of(k, a)], own_sem.at[2 * PARTS + a])

    def give_back(a, i):
        j, peer = chain_peer(i)
        return pltpu.make_async_remote_copy(
            src_ref=ready.at[a, j], dst_ref=out.at[rows_of(k, a)], send_sem=out_send.at[a, i - 1],
            recv_sem=out_recv.at[a, i - 1], device_id=peer, device_id_type=MESH)

    def given_back(a, i):
        j = (k + CHAIN - i) % CHAIN
        return pltpu.make_async_remote_copy(
            src_ref=ready.at[a, j], dst_ref=out.at[rows_of(j, a)], send_sem=out_send.at[a, i - 1],
            recv_sem=out_recv.at[a, i - 1], device_id=chain_peer(i)[1], device_id_type=MESH)

    for a in range(PARTS):
        @pl.loop(0, CHAIN - 1)
        def _(t):
            deal(tok, tok_slot, tok_send, tok_recv, a, crossing_first(t)).start()

        own_tok(a).start()
    for a in range(PARTS):
        @pl.loop(0, CHAIN - 1)
        def _(t):
            deal(cot, cot_slot, cot_send, cot_recv, a, crossing_first(t)).start()

        own_cot(a).start()
    zeros = jnp.zeros((4, ROWS, C), BF16)
    for layer in range(LAYERS):
        for a in range(PARTS):
            normed[layer, a, 0:4] = zeros
            normed[layer, a, 12:16] = zeros
    grad_hid[0:4] = zeros
    grad_hid[12:16] = zeros
    taps_acc[...] = jnp.zeros_like(taps_acc)
    taps_part[...] = jnp.zeros_like(taps_part)
    load_taps.wait()

    def forward(a):
        for layer in range(LAYERS):
            shift = 2**layer

            @pl.loop(0, CHAIN)
            def _(j):
                value = xin[a, j].astype(F32)
                mean = jnp.sum(value * value, axis=-1, keepdims=True) * (1.0 / C)
                inv = lax.rsqrt(mean + EPSILON)
                value = value * inv
                inverse[layer, a, j] = jnp.broadcast_to(inv, (ROWS, 128))
                normal[layer, a, j] = value
                normed[layer, a, 4 + j] = value.astype(BF16)

            @pl.loop(0, CHAIN)
            def _(j):
                hid = (
                    taps[layer, 0:1, :] * normed[layer, a, 4 + j - shift].astype(F32)
                    + taps[layer, 1:2, :] * normed[layer, a, 4 + j].astype(F32)
                    + taps[layer, 2:3, :] * normed[layer, a, 4 + j + shift].astype(F32)
                )
                square = hid * hid
                tanh = jnp.tanh(GELU_A * hid * (1.0 + GELU_B * square))
                half = 0.5 * (1.0 + tanh)
                active[layer, a, j] = (hid * half).astype(BF16)
                slope[layer, a, j] = half + (0.5 * GELU_A) * hid * (1.0 - tanh * tanh) * (1.0 + (3.0 * GELU_B) * square)

            if layer == LAYERS - 1:
                continue
            if a == 0:
                load(layer).wait()
            for n in range(C // COLS):
                cols = slice(n * COLS, (n + 1) * COLS)
                product = jnp.dot(active[layer, a].reshape(CHAIN * ROWS, C), w[layer, :, cols], preferred_element_type=F32)
                xin[a, :, :, cols] = (
                    xin[a, :, :, cols].astype(F32) + product.reshape(CHAIN, ROWS, COLS)).astype(BF16)

    def backward(a, layer):
        shift = 2**layer
        if a == 0 and layer == LAYERS - 1:
            load(layer).wait()
        for n in range(C // COLS):
            cols = slice(n * COLS, (n + 1) * COLS)
            spread = lax.dot_general(
                up[layer, a].reshape(CHAIN * ROWS, C), w[layer, cols, :], (((1,), (1,)), ((), ())),
                preferred_element_type=F32)
            grad_hid[4:12, :, cols] = (spread.reshape(CHAIN, ROWS, COLS) * slope[layer, a, :, :, cols]).astype(BF16)

        @pl.loop(0, CHAIN)
        def _(j):
            mid = grad_hid[4 + j].astype(F32)
            for t in range(3):
                term = mid * normed[layer, a, 4 + j + (t - 1) * shift].astype(F32)
                taps_acc[layer, t] += term[0:8] + term[8:16]
            moved = (
                taps[layer, 1:2, :] * mid
                + taps[layer, 0:1, :] * grad_hid[4 + j + shift].astype(F32)
                + taps[layer, 2:3, :] * grad_hid[4 + j - shift].astype(F32)
            )
            value = normal[layer, a, j]
            mean = jnp.sum(moved * value, axis=-1, keepdims=True) * (1.0 / C)
            before = up[layer, a, j].astype(F32) if layer == LAYERS - 1 else grad[j]
            after = before + inverse[layer, a, j, :, 0:1] * (moved - value * mean)
            if layer > 0:
                grad[j] = after
                up[layer - 1, a, j] = after.astype(BF16)
            else:
                ready[a, j] = after.astype(BF16)

    def point_terms(layer):
        rows = up[layer].reshape(PARTS * CHAIN * ROWS, C)
        acts = active[layer].reshape(PARTS * CHAIN * ROWS, C)
        over_rows = (((0,), (0,)), ((), ()))
        for m in range(2):
            some = acts[:, m * HALF:(m + 1) * HALF]
            product = lax.dot_general(rows[:, 0:HALF], some, over_rows, preferred_element_type=F32)
            terms[layer, 0, :, m] = product.astype(BF16).reshape(4, PIECE, HALF)
            product = lax.dot_general(some, rows[:, HALF:], over_rows, preferred_element_type=F32)
            terms[layer, 1, 2 * m:2 * m + 2] = product.astype(BF16).reshape(2, 2, PIECE, HALF)
        for t in range(3):
            line = jnp.sum(taps_acc[layer, t], axis=0, keepdims=True)
            for b in range(C // 128):
                row = (layer * 3 + t) * (C // 128) + b
                taps_part[row // 7, row % 7:row % 7 + 1, :] = line[:, b * 128:(b + 1) * 128]

    def to_sibling(layer):
        return pltpu.make_async_remote_copy(
            src_ref=terms.at[layer, 1 - core], dst_ref=sibling.at[layer], send_sem=core_sem.at[layer, 0],
            recv_sem=core_sem.at[layer, 1], device_id=(seq, dp + 1 - 2 * core), device_id_type=MESH)

    def around(layer, n):
        way = n % 2
        place = (p + 1 + 2 * way) % 4
        if n < 2:
            src, dst = summed.at[layer, (p + 2) % 4, way], half_way.at[layer, way]
        else:
            half = 1 - way if n < 4 else way
            src, dst = summed.at[layer, place, half], from_a.at[layer, way, half]
        return pltpu.make_async_remote_copy(
            src_ref=src, dst_ref=dst, send_sem=a_send.at[layer, n], recv_sem=a_recv.at[layer, n],
            device_id=first_peer(place), device_id_type=MESH)

    def parcel(layer, step, i):
        place, peer = step_peer(step, i)
        if step == 0:
            src, dst = to_b.at[layer, place], from_b.at[layer, i - 1]
        else:
            src, dst = to_z.at[layer, place], from_z.at[layer, i - 1]
        return pltpu.make_async_remote_copy(
            src_ref=src, dst_ref=dst, send_sem=red_send.at[layer, step, i - 1], recv_sem=red_recv.at[layer, step, i - 1],
            device_id=peer, device_id_type=MESH)

    def last_send_of(layer, e):
        return pltpu.make_async_remote_copy(
            src_ref=to_block.at[layer, e // 2], dst_ref=from_block.at[layer, block], send_sem=last_send.at[layer, e],
            recv_sem=last_recv.at[layer, block], device_id=owner(e), device_id_type=MESH)

    def last_arrival(layer, m):
        return pltpu.make_async_remote_copy(
            src_ref=to_block.at[layer, 0], dst_ref=from_block.at[layer, m], send_sem=last_send.at[layer, m],
            recv_sem=last_recv.at[layer, m], device_id=owner(m), device_id_type=MESH)

    def is_own(e):
        return jnp.logical_and(core == zh, e == h * 2 + core)

    def step_core(layer):
        to_sibling(layer).wait_recv()
        for q in (2, 1, 3, 0):
            place = (p + q) % 4
            summed[layer, place] = (
                terms[layer, core, place].astype(F32) + sibling[layer, place].astype(F32)).astype(BF16)
            if q == 2:
                around(layer, 0).start()
                around(layer, 1).start()
            if q == 1:
                around(layer, 2).start()
            if q == 3:
                around(layer, 3).start()

    def step_ring(layer):
        for way in range(2):
            around(layer, way).wait_recv()
            place = (p + 1 + 2 * way) % 4
            summed[layer, place, way] = (
                summed[layer, place, way].astype(F32) + half_way[layer, way].astype(F32)).astype(BF16)
            around(layer, 4 + way).start()

    def step_first(layer):
        for n in range(2, 6):
            around(layer, n).wait_recv()

        @pl.when(core == 0)
        def _():
            for half in range(2):
                for b in range(HALF // 128):
                    lanes = slice(b * 128, (b + 1) * 128)
                    total = (
                        summed[layer, p, half, :, lanes].astype(F32) + from_a[layer, 0, half, :, lanes].astype(F32)
                        + from_a[layer, 1, half, :, lanes].astype(F32))
                    total = jnp.concatenate([total, jnp.zeros((128 - PIECE, 128), F32)], axis=0)
                    turned[half * HALF + b * 128:half * HALF + (b + 1) * 128, :] = total.T

            @pl.loop(0, 32)
            def _(g):
                value = turned[pl.ds(pl.multiple_of(g * 24, 8), 24), :]
                value = jnp.concatenate([value, jnp.zeros((8, 128), F32)], axis=0)
                to_b[layer, g // 8, g % 4, (g // 4) % 2] = value.astype(BF16)

        @pl.when(core == 1)
        def _():
            for half in range(2):
                total = (
                    summed[layer, p, half].astype(F32) + from_a[layer, 0, half].astype(F32)
                    + from_a[layer, 1, half].astype(F32))
                for place in range(4):
                    value = total[:, place * PIECE:(place + 1) * PIECE]
                    value = jnp.concatenate([value, jnp.zeros((PIECE, 128 - PIECE), F32)], axis=1)
                    for g in range(4):
                        some = jnp.concatenate([value[g * 24:(g + 1) * 24], jnp.zeros((8, 128), F32)], axis=0)
                        to_b[layer, place, g, half] = some.astype(BF16)

        for i in range(1, 4):
            parcel(layer, 0, i).start()

    def step_second(layer):
        for i in range(1, 4):
            parcel(layer, 0, i).wait_recv()
        total = to_b[layer, r].astype(F32)
        for i in range(3):
            total = total + from_b[layer, i].astype(F32)
        to_z[layer] = total.astype(BF16)
        for i in range(1, 4):
            parcel(layer, 1, i).start()

    def step_z(layer):
        for i in range(1, 4):
            parcel(layer, 1, i).wait_recv()
        total = to_z[layer, c].astype(F32)
        for i in range(3):
            total = total + from_z[layer, i].astype(F32)
        to_block[layer] = total.astype(BF16)
        for e in range(4):
            @pl.when(is_own(e))
            def _():
                from_block[layer, block] = to_block[layer, e // 2]

            @pl.when(jnp.logical_not(is_own(e)))
            def _():
                last_send_of(layer, e).start()

    def step_last(layer):
        for m in range(4):
            @pl.when(jnp.logical_not(jnp.logical_and(core == zh, block == m)))
            def _():
                last_arrival(layer, m).wait_recv()
        total = from_block[layer, 0].astype(F32)
        for m in range(1, 4):
            total = total + from_block[layer, m].astype(F32)
        upper = jnp.broadcast_to(core, (24, 48)) > 0
        out_point[layer] = jnp.where(upper, total[0:24, 48:96], total[0:24, 0:48]) * factor

    def tap_partners(step):
        return range(1, 8 if step in (0, 4) else 4)

    def tap_copy(step, i):
        place, peer = tap_peer(step, i)
        if step == 0:
            src, dst = taps_part.at[place], taps_in.at[0, i - 1]
        elif step == 4:
            src, dst = taps_one.at[3], taps_all.at[dp % 8]
        else:
            src, dst = taps_one.at[step - 1], taps_in.at[step, i - 1]
        return pltpu.make_async_remote_copy(
            src_ref=src, dst_ref=dst, send_sem=tap_send.at[step, i - 1], recv_sem=tap_recv.at[step, i - 1],
            device_id=peer, device_id_type=MESH)

    def tap_gathered(i):
        place = (dp % 8 + 8 - i) % 8
        return pltpu.make_async_remote_copy(
            src_ref=taps_one.at[3], dst_ref=taps_all.at[place], send_sem=tap_send.at[4, i - 1],
            recv_sem=tap_recv.at[4, i - 1], device_id=tap_peer(4, i)[1], device_id_type=MESH)

    def tap_start(step):
        for i in tap_partners(step):
            tap_copy(step, i).start()

    def tap_step(step):
        for i in tap_partners(step):
            tap_copy(step, i).wait_recv()
        total = taps_part[dp % 8] if step == 0 else taps_one[step - 1]
        for i in tap_partners(step):
            total = total + taps_in[step, i - 1]
        taps_one[step] = total
        if step == 3:
            taps_all[dp % 8] = total
        tap_start(step + 1)

    def tap_last():
        for i in tap_partners(4):
            tap_gathered(i).wait_recv()
        for layer in range(LAYERS):
            for t in range(3):
                for b in range(C // 128):
                    row = (layer * 3 + t) * (C // 128) + b
                    out_taps[layer, t:t + 1, b * 128:(b + 1) * 128] = taps_all[row // 7, row % 7:row % 7 + 1, :] * factor

    def wait_dealt(src, slot, sends, recvs, own, a):
        @pl.loop(1, CHAIN)
        def _(i):
            dealt(src, slot, sends, recvs, a, i).wait_recv()

        own(a).wait()

    def send_back(a):
        @pl.loop(0, CHAIN - 1)
        def _(t):
            give_back(a, crossing_first(t)).start()

        own_out(a).start()

    for a in range(PARTS):
        wait_dealt(tok, tok_slot, tok_send, tok_recv, own_tok, a)
        forward(a)
    wait_dealt(cot, cot_slot, cot_send, cot_recv, own_cot, 0)
    for layer in (2, 1, 0):
        backward(0, layer)
    send_back(0)
    wait_dealt(cot, cot_slot, cot_send, cot_recv, own_cot, 1)
    backward(1, 2)
    point_terms(2)
    to_sibling(2).start()
    backward(1, 1)
    point_terms(1)
    to_sibling(1).start()
    step_core(2)
    backward(1, 0)
    send_back(1)
    point_terms(0)
    to_sibling(0).start()
    tap_start(0)
    step_core(1)
    step_ring(2)
    step_core(0)
    step_first(2)
    step_ring(1)
    tap_step(0)
    step_ring(0)
    step_first(1)
    step_second(2)
    tap_step(1)
    step_first(0)
    step_z(2)
    step_second(1)
    tap_step(2)
    step_second(0)
    step_z(1)
    step_last(2)
    tap_step(3)
    step_z(0)
    step_last(1)
    tap_last()
    step_last(0)

    for a in range(PARTS):
        own_out(a).wait()

        @pl.loop(1, CHAIN)
        def _(i):
            given_back(a, i).wait_recv()
            give_back(a, i).wait_send()
            deal(tok, tok_slot, tok_send, tok_recv, a, i).wait_send()
            deal(cot, cot_slot, cot_send, cot_recv, a, i).wait_send()
    for layer in range(LAYERS):
        to_sibling(layer).wait_send()
        for n in range(6):
            around(layer, n).wait_send()
        for step in range(2):
            for i in range(1, 4):
                parcel(layer, step, i).wait_send()
        for e in range(4):
            @pl.when(jnp.logical_not(is_own(e)))
            def _():
                last_send_of(layer, e).wait_send()
    for step in range(5):
        for i in tap_partners(step):
            tap_copy(step, i).wait_send()


def local(factor, tokens, cotangent, conv_kernel, point_weight):
    any_space = pl.BlockSpec(memory_space=pl.ANY)
    vmem = pl.BlockSpec(memory_space=pltpu.VMEM)
    part = (PARTS, CHAIN, ROWS, C)
    scratch = [
        pltpu.VMEM(part, BF16),
        pltpu.VMEM((LAYERS, PARTS, CHAIN + 8, ROWS, C), BF16),
        pltpu.VMEM((LAYERS,) + part, F32),
        pltpu.VMEM((LAYERS, PARTS, CHAIN, ROWS, 128), F32),
        pltpu.VMEM((LAYERS,) + part, F32),
        pltpu.VMEM((LAYERS,) + part, BF16),
        pltpu.VMEM((LAYERS,) + part, BF16),
        pltpu.VMEM((CHAIN, ROWS, C), F32),
        pltpu.VMEM((CHAIN + 8, ROWS, C), BF16),
        pltpu.VMEM(part, BF16),
        pltpu.VMEM((LAYERS, C, C), BF16),
        pltpu.VMEM((LAYERS, 3, C), F32),
        pltpu.VMEM((LAYERS, 2, 4, 2, PIECE, HALF), BF16),
        pltpu.VMEM((LAYERS, 4, 2, PIECE, HALF), BF16),
        pltpu.VMEM((LAYERS, 4, 2, PIECE, HALF), BF16),
        pltpu.VMEM((LAYERS, 2, PIECE, HALF), BF16),
        pltpu.VMEM((LAYERS, 2, 2, PIECE, HALF), BF16),
        pltpu.VMEM((C, 128), F32),
        pltpu.VMEM((LAYERS, 4, 4, 2, 32, 128), BF16),
        pltpu.VMEM((LAYERS, 3, 4, 2, 32, 128), BF16),
        pltpu.VMEM((LAYERS, 4, 2, 32, 128), BF16),
        pltpu.VMEM((LAYERS, 3, 2, 32, 128), BF16),
        pltpu.VMEM((LAYERS, 2, 32, 128), BF16),
        pltpu.VMEM((LAYERS, 4, 32, 128), BF16),
        pltpu.VMEM((LAYERS, 3, 8, C), F32),
        pltpu.VMEM((8, 8, 128), F32),
        pltpu.VMEM((4, 8, 128), F32),
        pltpu.VMEM((4, 7, 8, 128), F32),
        pltpu.VMEM((8, 8, 128), F32),
        pltpu.SemaphoreType.DMA((PARTS, CHAIN - 1)),
        pltpu.SemaphoreType.DMA((PARTS, CHAIN - 1)),
        pltpu.SemaphoreType.DMA((PARTS, CHAIN - 1)),
        pltpu.SemaphoreType.DMA((PARTS, CHAIN - 1)),
        pltpu.SemaphoreType.DMA((PARTS, CHAIN - 1)),
        pltpu.SemaphoreType.DMA((PARTS, CHAIN - 1)),
        pltpu.SemaphoreType.DMA((3 * PARTS,)),
        pltpu.SemaphoreType.DMA((LAYERS + 1,)),
        pltpu.SemaphoreType.DMA((LAYERS, 2)),
        pltpu.SemaphoreType.DMA((LAYERS, 6)),
        pltpu.SemaphoreType.DMA((LAYERS, 6)),
        pltpu.SemaphoreType.DMA((LAYERS, 2, 3)),
        pltpu.SemaphoreType.DMA((LAYERS, 2, 3)),
        pltpu.SemaphoreType.DMA((LAYERS, 4)),
        pltpu.SemaphoreType.DMA((LAYERS, 4)),
        pltpu.SemaphoreType.DMA((5, 7)),
        pltpu.SemaphoreType.DMA((5, 7)),
    ]
    out, out_point, out_taps = pl.pallas_call(
        functools.partial(kernel, factor),
        out_shape=(
            jax.ShapeDtypeStruct((SLAB, C), BF16),
            jax.ShapeDtypeStruct((LAYERS, 24, 48), F32),
            jax.ShapeDtypeStruct((LAYERS, 3, C), F32),
        ),
        in_specs=[any_space] * 4,
        out_specs=(any_space, vmem, vmem),
        scratch_shapes=scratch,
        compiler_params=pltpu.CompilerParams(collective_id=0, has_side_effects=True, vmem_limit_bytes=60 * 2**20),
        cost_estimate=pl.CostEstimate(flops=2 * 9 * SLAB * C * C, bytes_accessed=6 * 2**20, transcendentals=LAYERS * SLAB * C),
    )(tokens[0], cotangent[0], conv_kernel, point_weight)
    return out[None], out_point, out_taps


def solution(mesh):
    factor = 1.0 / math.sqrt(mesh.shape["seq"] * mesh.shape["dp"] * SLAB)
    P = jax.sharding.PartitionSpec
    return jax.shard_map(
        functools.partial(local, factor),
        mesh=mesh,
        in_specs=(P("dp", "seq", None), P("dp", "seq", None), P(), P()),
        out_specs=(P("dp", "seq", None), P(None, "seq", "dp"), P()),
        check_vma=False,
    )
```

```python
import functools
import math

import jax
import jax.numpy as jnp
from jax import lax
from jax.experimental import pallas as pl
from jax.experimental.pallas import tpu as pltpu

EPSILON = 1e-06
MESH = pl.DeviceIdType.MESH
F32 = jnp.float32
BF16 = jnp.bfloat16

C = 768
LAYERS = 3
CHAIN = 8
ROWS = 16
PARTS = 2
SLAB = 256
COLS = 256
HALF = C // 2
PIECE = 96
GELU_A = math.sqrt(2.0 / math.pi)
GELU_B = 0.044715


def kernel(factor, tok, cot, taps_hbm, weight, out, out_point, out_taps, *scratch):
    (xin, normed, normal, inverse, slope, active, up, grad, grad_hid, ready, w, taps, terms, sibling, summed, half_way, from_a,
     turned, to_b, from_b, to_z, from_z, taps_acc, taps_part, taps_one, taps_in, taps_all,
     tok_send, tok_recv, cot_send, cot_recv, out_send, out_recv, own_sem, w_sem, core_sem, a_send, a_recv, red_send, red_recv,
     z_send, z_recv, tap_send, tap_recv, round_sem, pair_sem) = scratch
    seq = lax.axis_index("seq")
    dp = lax.axis_index("dp")
    k, c = seq // 4, seq % 4
    y, h = seq // 8, (seq // 4) % 2
    zh, x, core = dp // 8, (dp // 2) % 4, dp % 2
    block = zh * 2 + h
    p = x + core * (y - x)
    r = y + core * (x - y)

    def chain_peer(i):
        j = (k + i) % CHAIN
        return j, (j * 4 + c, dp)

    def first_peer(place):
        return seq + core * (place - y) * 8, dp + (1 - core) * (place - x) * 2

    def second_peer(i):
        place = (r + i) % 4
        return place, (seq + (1 - core) * (place - y) * 8, dp + core * (place - x) * 2)

    z = zh * 8 + h * 4 + c

    def z_device(place, of_core):
        return y * 8 + place % 8, (place // 8) * 8 + x * 2 + of_core

    def tap_peer(step, i):
        if step in (0, 3):
            place = (dp % 8 + i) % 8
            return place, (seq, zh * 8 + place)
        if step == 1:
            place = (y + i) % 4
            return place, (place * 8 + h * 4 + c, dp)
        place = (z + i) % 16
        return place, z_device(place, core)

    barrier = pltpu.get_barrier_semaphore()

    def greet(peer):
        pl.semaphore_signal(barrier, inc=1, device_id=peer, device_id_type=MESH)

    @pl.loop(1, CHAIN)
    def _(i):
        greet(chain_peer(i)[1])
        greet(tap_peer(0, i)[1])

    above, below = z_device((z + 1) % 16, core), z_device((z + 15) % 16, core)
    greet(above)
    greet(below)

    def load(layer):
        return pltpu.make_async_copy(weight.at[layer], w.at[layer], w_sem.at[layer])

    load_taps = pltpu.make_async_copy(taps_hbm, taps, w_sem.at[LAYERS])
    load_taps.start()
    for layer in range(LAYERS):
        load(layer).start()

    pl.semaphore_wait(barrier, 16)

    def rows_of(j, a):
        return pl.ds(pl.multiple_of(j * (PARTS * ROWS) + a * ROWS, ROWS), ROWS)

    def crossing_first(t):
        return 2 * t + 1 - 7 * (t // 4)

    def deal(src, dst_of, send, recv, a, i):
        j, peer = chain_peer(i)
        return pltpu.make_async_remote_copy(
            src_ref=src.at[rows_of(j, a)], dst_ref=dst_of(a, k), send_sem=send.at[a, i - 1], recv_sem=recv.at[a, i - 1],
            device_id=peer, device_id_type=MESH)

    def dealt(src, dst_of, send, recv, a, i):
        j = (k + CHAIN - i) % CHAIN
        return pltpu.make_async_remote_copy(
            src_ref=src.at[rows_of(j, a)], dst_ref=dst_of(a, j), send_sem=send.at[a, i - 1], recv_sem=recv.at[a, i - 1],
            device_id=chain_peer(i)[1], device_id_type=MESH)

    def tok_slot(a, j):
        return xin.at[a, j]

    def cot_slot(a, j):
        return up.at[LAYERS - 1, a, j]

    def own_tok(a):
        return pltpu.make_async_copy(tok.at[rows_of(k, a)], xin.at[a, k], own_sem.at[a])

    def own_cot(a):
        return pltpu.make_async_copy(cot.at[rows_of(k, a)], up.at[LAYERS - 1, a, k], own_sem.at[PARTS + a])

    def own_out(a):
        return pltpu.make_async_copy(ready.at[a, k], out.at[rows_of(k, a)], own_sem.at[2 * PARTS + a])

    def give_back(a, i):
        j, peer = chain_peer(i)
        return pltpu.make_async_remote_copy(
            src_ref=ready.at[a, j], dst_ref=out.at[rows_of(k, a)], send_sem=out_send.at[a, i - 1],
            recv_sem=out_recv.at[a, i - 1], device_id=peer, device_id_type=MESH)

    def given_back(a, i):
        j = (k + CHAIN - i) % CHAIN
        return pltpu.make_async_remote_copy(
            src_ref=ready.at[a, j], dst_ref=out.at[rows_of(j, a)], send_sem=out_send.at[a, i - 1],
            recv_sem=out_recv.at[a, i - 1], device_id=chain_peer(i)[1], device_id_type=MESH)

    for a in range(PARTS):
        @pl.loop(0, CHAIN - 1)
        def _(t):
            deal(tok, tok_slot, tok_send, tok_recv, a, crossing_first(t)).start()

        own_tok(a).start()
    for a in range(PARTS):
        @pl.loop(0, CHAIN - 1)
        def _(t):
            deal(cot, cot_slot, cot_send, cot_recv, a, crossing_first(t)).start()

        own_cot(a).start()
    @pl.loop(0, 8)
    def _(t):
        pl.semaphore_signal(round_sem.at[t, 0], inc=1, device_id=above, device_id_type=MESH)
        pl.semaphore_signal(round_sem.at[t, 1], inc=1, device_id=below, device_id_type=MESH)
        pl.semaphore_wait(round_sem.at[t, 0], 1)
        pl.semaphore_wait(round_sem.at[t, 1], 1)

    pl.semaphore_signal(pair_sem, inc=1, device_id=(seq, dp + 1 - 2 * core), device_id_type=MESH)
    pl.semaphore_wait(pair_sem, 1)

    zeros = jnp.zeros((4, ROWS, C), BF16)
    for layer in range(LAYERS):
        for a in range(PARTS):
            normed[layer, a, 0:4] = zeros
            normed[layer, a, 12:16] = zeros
    grad_hid[0:4] = zeros
    grad_hid[12:16] = zeros
    taps_acc[...] = jnp.zeros_like(taps_acc)
    taps_part[...] = jnp.zeros_like(taps_part)
    load_taps.wait()

    def forward(a):
        for layer in range(LAYERS):
            shift = 2**layer

            @pl.loop(0, CHAIN)
            def _(j):
                value = xin[a, j].astype(F32)
                mean = jnp.sum(value * value, axis=-1, keepdims=True) * (1.0 / C)
                inv = lax.rsqrt(mean + EPSILON)
                value = value * inv
                inverse[layer, a, j] = jnp.broadcast_to(inv, (ROWS, 128))
                normal[layer, a, j] = value
                normed[layer, a, 4 + j] = value.astype(BF16)

            @pl.loop(0, CHAIN)
            def _(j):
                hid = (
                    taps[layer, 0:1, :] * normed[layer, a, 4 + j - shift].astype(F32)
                    + taps[layer, 1:2, :] * normed[layer, a, 4 + j].astype(F32)
                    + taps[layer, 2:3, :] * normed[layer, a, 4 + j + shift].astype(F32)
                )
                square = hid * hid
                tanh = jnp.tanh(GELU_A * hid * (1.0 + GELU_B * square))
                half = 0.5 * (1.0 + tanh)
                active[layer, a, j] = (hid * half).astype(BF16)
                slope[layer, a, j] = half + (0.5 * GELU_A) * hid * (1.0 - tanh * tanh) * (1.0 + (3.0 * GELU_B) * square)

            if layer == LAYERS - 1:
                continue
            if a == 0:
                load(layer).wait()
            for n in range(C // COLS):
                cols = slice(n * COLS, (n + 1) * COLS)
                product = jnp.dot(active[layer, a].reshape(CHAIN * ROWS, C), w[layer, :, cols], preferred_element_type=F32)
                xin[a, :, :, cols] = (
                    xin[a, :, :, cols].astype(F32) + product.reshape(CHAIN, ROWS, COLS)).astype(BF16)

    def backward(a, layer):
        shift = 2**layer
        if a == 0 and layer == LAYERS - 1:
            load(layer).wait()
        for n in range(C // COLS):
            cols = slice(n * COLS, (n + 1) * COLS)
            spread = lax.dot_general(
                up[layer, a].reshape(CHAIN * ROWS, C), w[layer, cols, :], (((1,), (1,)), ((), ())),
                preferred_element_type=F32)
            grad_hid[4:12, :, cols] = (spread.reshape(CHAIN, ROWS, COLS) * slope[layer, a, :, :, cols]).astype(BF16)

        @pl.loop(0, CHAIN)
        def _(j):
            mid = grad_hid[4 + j].astype(F32)
            for t in range(3):
                term = mid * normed[layer, a, 4 + j + (t - 1) * shift].astype(F32)
                taps_acc[layer, t] += term[0:8] + term[8:16]
            moved = (
                taps[layer, 1:2, :] * mid
                + taps[layer, 0:1, :] * grad_hid[4 + j + shift].astype(F32)
                + taps[layer, 2:3, :] * grad_hid[4 + j - shift].astype(F32)
            )
            value = normal[layer, a, j]
            mean = jnp.sum(moved * value, axis=-1, keepdims=True) * (1.0 / C)
            before = up[layer, a, j].astype(F32) if layer == LAYERS - 1 else grad[j]
            after = before + inverse[layer, a, j, :, 0:1] * (moved - value * mean)
            if layer > 0:
                grad[j] = after
                up[layer - 1, a, j] = after.astype(BF16)
            else:
                ready[a, j] = after.astype(BF16)

    def point_terms(layer):
        rows = up[layer].reshape(PARTS * CHAIN * ROWS, C)
        acts = active[layer].reshape(PARTS * CHAIN * ROWS, C)
        over_rows = (((0,), (0,)), ((), ()))
        for m in range(2):
            some = acts[:, m * HALF:(m + 1) * HALF]
            product = lax.dot_general(rows[:, 0:HALF], some, over_rows, preferred_element_type=F32)
            terms[layer, 0, :, m] = product.astype(BF16).reshape(4, PIECE, HALF)
            product = lax.dot_general(some, rows[:, HALF:], over_rows, preferred_element_type=F32)
            terms[layer, 1, 2 * m:2 * m + 2] = product.astype(BF16).reshape(2, 2, PIECE, HALF)

    def tap_terms():
        for layer in range(LAYERS):
            for t in range(3):
                line = jnp.sum(taps_acc[layer, t], axis=0, keepdims=True)
                for b in range(C // 128):
                    row = (layer * 3 + t) * (C // 128) + b
                    taps_part[row // 7, row % 7:row % 7 + 1, :] = line[:, b * 128:(b + 1) * 128]

    def to_sibling(layer):
        return pltpu.make_async_remote_copy(
            src_ref=terms.at[layer, 1 - core], dst_ref=sibling.at[layer], send_sem=core_sem.at[layer, 0],
            recv_sem=core_sem.at[layer, 1], device_id=(seq, dp + 1 - 2 * core), device_id_type=MESH)

    def around(layer, n):
        way = n % 2
        place = (p + 1 + 2 * way) % 4
        if n < 2:
            src, dst = summed.at[layer, (p + 2) % 4, way], half_way.at[layer, way]
        else:
            half = 1 - way if n < 4 else way
            src, dst = summed.at[layer, place, half], from_a.at[layer, way, half]
        return pltpu.make_async_remote_copy(
            src_ref=src, dst_ref=dst, send_sem=a_send.at[layer, n], recv_sem=a_recv.at[layer, n],
            device_id=first_peer(place), device_id_type=MESH)

    def parcel(layer, i):
        place, peer = second_peer(i)
        return pltpu.make_async_remote_copy(
            src_ref=to_b.at[layer, place], dst_ref=from_b.at[layer, i - 1], send_sem=red_send.at[layer, i - 1],
            recv_sem=red_recv.at[layer, i - 1], device_id=peer, device_id_type=MESH)

    def to_owner(e):
        place = e // 2
        return pltpu.make_async_remote_copy(
            src_ref=to_z.at[e % 2, place], dst_ref=from_z.at[z], send_sem=z_send.at[e],
            recv_sem=z_recv.at[z], device_id=z_device(core * 8 + place, e % 2), device_id_type=MESH)

    def z_arrival(m):
        return pltpu.make_async_remote_copy(
            src_ref=to_z.at[0, 0], dst_ref=from_z.at[m], send_sem=z_send.at[m],
            recv_sem=z_recv.at[m], device_id=z_device(m, zh), device_id_type=MESH)

    def is_own(e):
        return jnp.logical_and(core == zh, e == (h * 4 + c) * 2 + core)

    def step_core(layer):
        to_sibling(layer).wait_recv()
        for q in (2, 1, 3, 0):
            place = (p + q) % 4
            summed[layer, place] = (
                terms[layer, core, place].astype(F32) + sibling[layer, place].astype(F32)).astype(BF16)
            if q == 2:
                around(layer, 0).start()
                around(layer, 1).start()
            if q == 1:
                around(layer, 2).start()
            if q == 3:
                around(layer, 3).start()

    def step_ring(layer):
        for way in range(2):
            around(layer, way).wait_recv()
            place = (p + 1 + 2 * way) % 4
            summed[layer, place, way] = (
                summed[layer, place, way].astype(F32) + half_way[layer, way].astype(F32)).astype(BF16)
            around(layer, 4 + way).start()

    def step_first(layer):
        for n in range(2, 6):
            around(layer, n).wait_recv()

        @pl.when(core == 0)
        def _():
            for half in range(2):
                for b in range(HALF // 128):
                    lanes = slice(b * 128, (b + 1) * 128)
                    total = (
                        summed[layer, p, half, :, lanes].astype(F32) + from_a[layer, 0, half, :, lanes].astype(F32)
                        + from_a[layer, 1, half, :, lanes].astype(F32))
                    total = jnp.concatenate([total, jnp.zeros((128 - PIECE, 128), F32)], axis=0)
                    turned[half * HALF + b * 128:half * HALF + (b + 1) * 128, :] = total.T

            @pl.loop(0, 32)
            def _(g):
                value = turned[pl.ds(pl.multiple_of(g * 24, 8), 24), :]
                value = jnp.concatenate([value, jnp.zeros((8, 128), F32)], axis=0)
                to_b[layer, g // 8, g % 8] = value.astype(BF16)

        @pl.when(core == 1)
        def _():
            for half in range(2):
                total = (
                    summed[layer, p, half].astype(F32) + from_a[layer, 0, half].astype(F32)
                    + from_a[layer, 1, half].astype(F32))
                for place in range(4):
                    value = total[:, place * PIECE:(place + 1) * PIECE]
                    value = jnp.concatenate([value, jnp.zeros((PIECE, 128 - PIECE), F32)], axis=1)
                    for g in range(4):
                        some = jnp.concatenate([value[g * 24:(g + 1) * 24], jnp.zeros((8, 128), F32)], axis=0)
                        to_b[layer, place, half * 4 + g] = some.astype(BF16)

        for i in range(1, 4):
            parcel(layer, i).start()

    def step_second():
        totals = []
        for layer in range(LAYERS):
            for i in range(1, 4):
                parcel(layer, i).wait_recv()
            total = to_b[layer, r, :, 0:24].astype(F32)
            for i in range(3):
                total = total + from_b[layer, i, :, 0:24].astype(F32)
            totals.append(total.reshape(8 * 24, 128))
        for of_core in range(2):
            first = of_core * 48
            top = jnp.concatenate(
                [totals[2][:, first:first + 48], totals[1][:, first:first + 48], totals[0][:, first:first + 32]], axis=1)
            rest = totals[0][:, first + 32:first + 48].reshape(8, 3, 8, 16)
            rest = [rest[:, g].reshape(64, 16) for g in range(3)] + [jnp.zeros((64, 80), F32)]
            rest = jnp.concatenate(rest, axis=1)
            whole = jnp.concatenate([top.reshape(8, 24, 128), rest.reshape(8, 8, 128)], axis=1)
            to_z[of_core] = whole.astype(BF16)

        @pl.loop(0, 16)
        def _(e):
            @pl.when(is_own(e))
            def _():
                from_z[z] = to_z[core, h * 4 + c]

            @pl.when(jnp.logical_not(is_own(e)))
            def _():
                to_owner(e).start()

    def step_last():
        @pl.loop(0, 16)
        def _(m):
            @pl.when(jnp.logical_not(jnp.logical_and(core == zh, z == m)))
            def _():
                z_arrival(m).wait_recv()

        total = from_z[0].astype(F32)
        for m in range(1, 16):
            total = total + from_z[m].astype(F32)
        total = total * factor
        out_point[2] = total[0:24, 0:48]
        out_point[1] = total[0:24, 48:96]
        rest = jnp.concatenate([total[24:32, g * 16:(g + 1) * 16] for g in range(3)], axis=0)
        out_point[0] = jnp.concatenate([total[0:24, 96:128], rest], axis=1)

    tap_partners = (range(1, 8), range(1, 4), range(1, 16), range(1, 8))

    def tap_copy(step, i):
        place, peer = tap_peer(step, i)
        if step == 0:
            src, dst = taps_part.at[place], taps_in.at[0, i - 1]
        elif step == 3:
            src, dst = taps_one.at[2], taps_all.at[dp % 8]
        else:
            src, dst = taps_one.at[step - 1], taps_in.at[step, i - 1]
        return pltpu.make_async_remote_copy(
            src_ref=src, dst_ref=dst, send_sem=tap_send.at[step, i - 1], recv_sem=tap_recv.at[step, i - 1],
            device_id=peer, device_id_type=MESH)

    def tap_gathered(i):
        place = (dp % 8 + 8 - i) % 8
        return pltpu.make_async_remote_copy(
            src_ref=taps_one.at[2], dst_ref=taps_all.at[place], send_sem=tap_send.at[3, i - 1],
            recv_sem=tap_recv.at[3, i - 1], device_id=tap_peer(3, i)[1], device_id_type=MESH)

    def tap_start(step):
        @pl.loop(tap_partners[step].start, tap_partners[step].stop)
        def _(i):
            tap_copy(step, i).start()

    def tap_step(step):
        @pl.loop(tap_partners[step].start, tap_partners[step].stop)
        def _(i):
            tap_copy(step, i).wait_recv()

        total = taps_part[dp % 8] if step == 0 else taps_one[step - 1]
        for i in tap_partners[step]:
            total = total + taps_in[step, i - 1]
        taps_one[step] = total
        if step == 2:
            taps_all[dp % 8] = total
        tap_start(step + 1)

    def tap_last():
        @pl.loop(1, 8)
        def _(i):
            tap_gathered(i).wait_recv()

        for layer in range(LAYERS):
            for t in range(3):
                for b in range(C // 128):
                    row = (layer * 3 + t) * (C // 128) + b
                    out_taps[layer, t:t + 1, b * 128:(b + 1) * 128] = taps_all[row // 7, row % 7:row % 7 + 1, :] * factor

    def wait_dealt(src, slot, sends, recvs, own, a):
        @pl.loop(1, CHAIN)
        def _(i):
            dealt(src, slot, sends, recvs, a, i).wait_recv()

        own(a).wait()

    def send_back(a):
        @pl.loop(0, CHAIN - 1)
        def _(t):
            give_back(a, crossing_first(t)).start()

        own_out(a).start()

    for a in range(PARTS):
        wait_dealt(tok, tok_slot, tok_send, tok_recv, own_tok, a)
        forward(a)
    wait_dealt(cot, cot_slot, cot_send, cot_recv, own_cot, 0)
    for layer in (2, 1, 0):
        backward(0, layer)
    send_back(0)
    wait_dealt(cot, cot_slot, cot_send, cot_recv, own_cot, 1)
    point_terms(2)
    to_sibling(2).start()
    backward(1, 2)
    point_terms(1)
    to_sibling(1).start()
    step_core(2)
    backward(1, 1)
    point_terms(0)
    to_sibling(0).start()
    step_core(1)
    step_ring(2)
    backward(1, 0)
    send_back(1)
    tap_terms()
    tap_start(0)
    step_core(0)
    step_ring(1)
    step_first(2)
    step_ring(0)
    tap_step(0)
    step_first(1)
    step_first(0)
    tap_step(1)
    step_second()
    tap_step(2)
    step_last()
    tap_last()

    for a in range(PARTS):
        own_out(a).wait()

        @pl.loop(1, CHAIN)
        def _(i):
            given_back(a, i).wait_recv()
            give_back(a, i).wait_send()
            deal(tok, tok_slot, tok_send, tok_recv, a, i).wait_send()
            deal(cot, cot_slot, cot_send, cot_recv, a, i).wait_send()
    for layer in range(LAYERS):
        to_sibling(layer).wait_send()
        for n in range(6):
            around(layer, n).wait_send()
        for i in range(1, 4):
            parcel(layer, i).wait_send()

    @pl.loop(0, 16)
    def _(e):
        @pl.when(jnp.logical_not(is_own(e)))
        def _():
            to_owner(e).wait_send()

    for step in range(4):
        @pl.loop(tap_partners[step].start, tap_partners[step].stop)
        def _(i):
            tap_copy(step, i).wait_send()


def local(factor, tokens, cotangent, conv_kernel, point_weight):
    any_space = pl.BlockSpec(memory_space=pl.ANY)
    vmem = pl.BlockSpec(memory_space=pltpu.VMEM)
    part = (PARTS, CHAIN, ROWS, C)
    scratch = [
        pltpu.VMEM(part, BF16),
        pltpu.VMEM((LAYERS, PARTS, CHAIN + 8, ROWS, C), BF16),
        pltpu.VMEM((LAYERS,) + part, F32),
        pltpu.VMEM((LAYERS, PARTS, CHAIN, ROWS, 128), F32),
        pltpu.VMEM((LAYERS,) + part, F32),
        pltpu.VMEM((LAYERS,) + part, BF16),
        pltpu.VMEM((LAYERS,) + part, BF16),
        pltpu.VMEM((CHAIN, ROWS, C), F32),
        pltpu.VMEM((CHAIN + 8, ROWS, C), BF16),
        pltpu.VMEM(part, BF16),
        pltpu.VMEM((LAYERS, C, C), BF16),
        pltpu.VMEM((LAYERS, 3, C), F32),
        pltpu.VMEM((LAYERS, 2, 4, 2, PIECE, HALF), BF16),
        pltpu.VMEM((LAYERS, 4, 2, PIECE, HALF), BF16),
        pltpu.VMEM((LAYERS, 4, 2, PIECE, HALF), BF16),
        pltpu.VMEM((LAYERS, 2, PIECE, HALF), BF16),
        pltpu.VMEM((LAYERS, 2, 2, PIECE, HALF), BF16),
        pltpu.VMEM((C, 128), F32),
        pltpu.VMEM((LAYERS, 4, 8, 32, 128), BF16),
        pltpu.VMEM((LAYERS, 3, 8, 32, 128), BF16),
        pltpu.VMEM((2, 8, 32, 128), BF16),
        pltpu.VMEM((16, 32, 128), BF16),
        pltpu.VMEM((LAYERS, 3, 8, C), F32),
        pltpu.VMEM((8, 8, 128), F32),
        pltpu.VMEM((3, 8, 128), F32),
        pltpu.VMEM((3, 15, 8, 128), F32),
        pltpu.VMEM((8, 8, 128), F32),
        pltpu.SemaphoreType.DMA((PARTS, CHAIN - 1)),
        pltpu.SemaphoreType.DMA((PARTS, CHAIN - 1)),
        pltpu.SemaphoreType.DMA((PARTS, CHAIN - 1)),
        pltpu.SemaphoreType.DMA((PARTS, CHAIN - 1)),
        pltpu.SemaphoreType.DMA((PARTS, CHAIN - 1)),
        pltpu.SemaphoreType.DMA((PARTS, CHAIN - 1)),
        pltpu.SemaphoreType.DMA((3 * PARTS,)),
        pltpu.SemaphoreType.DMA((LAYERS + 1,)),
        pltpu.SemaphoreType.DMA((LAYERS, 2)),
        pltpu.SemaphoreType.DMA((LAYERS, 6)),
        pltpu.SemaphoreType.DMA((LAYERS, 6)),
        pltpu.SemaphoreType.DMA((LAYERS, 3)),
        pltpu.SemaphoreType.DMA((LAYERS, 3)),
        pltpu.SemaphoreType.DMA((16,)),
        pltpu.SemaphoreType.DMA((16,)),
        pltpu.SemaphoreType.DMA((4, 15)),
        pltpu.SemaphoreType.DMA((4, 15)),
        pltpu.SemaphoreType.REGULAR((8, 2)),
        pltpu.SemaphoreType.REGULAR,
    ]
    out, out_point, out_taps = pl.pallas_call(
        functools.partial(kernel, factor),
        out_shape=(
            jax.ShapeDtypeStruct((SLAB, C), BF16),
            jax.ShapeDtypeStruct((LAYERS, 24, 48), F32),
            jax.ShapeDtypeStruct((LAYERS, 3, C), F32),
        ),
        in_specs=[any_space] * 4,
        out_specs=(any_space, vmem, vmem),
        scratch_shapes=scratch,
        compiler_params=pltpu.CompilerParams(collective_id=0, has_side_effects=True, vmem_limit_bytes=60 * 2**20),
        cost_estimate=pl.CostEstimate(flops=2 * 9 * SLAB * C * C, bytes_accessed=6 * 2**20, transcendentals=LAYERS * SLAB * C),
    )(tokens[0], cotangent[0], conv_kernel, point_weight)
    return out[None], out_point, out_taps


def solution(mesh):
    factor = 1.0 / math.sqrt(mesh.shape["seq"] * mesh.shape["dp"] * SLAB)
    P = jax.sharding.PartitionSpec
    return jax.shard_map(
        functools.partial(local, factor),
        mesh=mesh,
        in_specs=(P("dp", "seq", None), P("dp", "seq", None), P(), P()),
        out_specs=(P("dp", "seq", None), P(None, "seq", "dp"), P()),
        check_vma=False,
    )
```

```python
import functools
import math

import jax
import jax.numpy as jnp
from jax import lax
from jax.experimental import pallas as pl
from jax.experimental.pallas import tpu as pltpu

EPSILON = 1e-06
MESH = pl.DeviceIdType.MESH
F32 = jnp.float32
BF16 = jnp.bfloat16

C = 768
LAYERS = 3
CHAIN = 8
ROWS = 16
PARTS = 2
SLAB = 256
COLS = 256
HALF = C // 2
PIECE = 96
GELU_A = math.sqrt(2.0 / math.pi)
GELU_B = 0.044715


def kernel(factor, tok, cot, taps_hbm, weight, out, out_point, out_taps, *scratch):
    (xin, normed, normal, inverse, slope, active, up, grad, grad_hid, ready, w, taps, sib_active, sib_up, summed, half_way, from_a,
     to_b, from_b, to_z, from_z, taps_acc, taps_part, taps_one, taps_in, taps_all,
     tok_send, tok_recv, cot_send, cot_recv, out_send, out_recv, own_sem, w_sem, act_sem, up_sem, a_send, a_recv, red_send, red_recv,
     z_send, z_recv, tap_send, tap_recv, round_sem, pair_sem) = scratch
    seq = lax.axis_index("seq")
    dp = lax.axis_index("dp")
    k, c = seq // 4, seq % 4
    y, h = seq // 8, (seq // 4) % 2
    zh, x, core = dp // 8, (dp // 2) % 4, dp % 2
    block = zh * 2 + h
    p = x + core * (y - x)
    r = y + core * (x - y)

    def chain_peer(i):
        j = (k + i) % CHAIN
        return j, (j * 4 + c, dp)

    def first_peer(place):
        return seq + core * (place - y) * 8, dp + (1 - core) * (place - x) * 2

    def second_peer(i):
        place = (r + i) % 4
        return place, (seq + (1 - core) * (place - y) * 8, dp + core * (place - x) * 2)

    z = zh * 8 + h * 4 + c

    def z_device(place, of_core):
        return y * 8 + place % 8, (place // 8) * 8 + x * 2 + of_core

    def tap_peer(step, i):
        if step in (0, 3):
            place = (dp % 8 + i) % 8
            return place, (seq, zh * 8 + place)
        if step == 1:
            place = (y + i) % 4
            return place, (place * 8 + h * 4 + c, dp)
        place = (z + i) % 16
        return place, z_device(place, core)

    barrier = pltpu.get_barrier_semaphore()

    def greet(peer):
        pl.semaphore_signal(barrier, inc=1, device_id=peer, device_id_type=MESH)

    @pl.loop(1, CHAIN)
    def _(i):
        greet(chain_peer(i)[1])
        greet(tap_peer(0, i)[1])

    above, below = z_device((z + 1) % 16, core), z_device((z + 15) % 16, core)
    greet(above)
    greet(below)

    def load(layer):
        return pltpu.make_async_copy(weight.at[layer], w.at[layer], w_sem.at[layer])

    load_taps = pltpu.make_async_copy(taps_hbm, taps, w_sem.at[LAYERS])
    load_taps.start()
    for layer in range(LAYERS):
        load(layer).start()

    pl.semaphore_wait(barrier, 16)

    def rows_of(j, a):
        return pl.ds(pl.multiple_of(j * (PARTS * ROWS) + a * ROWS, ROWS), ROWS)

    def crossing_first(t):
        return 2 * t + 1 - 7 * (t // 4)

    def deal(src, dst_of, send, recv, a, i):
        j, peer = chain_peer(i)
        return pltpu.make_async_remote_copy(
            src_ref=src.at[rows_of(j, a)], dst_ref=dst_of(a, k), send_sem=send.at[a, i - 1], recv_sem=recv.at[a, i - 1],
            device_id=peer, device_id_type=MESH)

    def dealt(src, dst_of, send, recv, a, i):
        j = (k + CHAIN - i) % CHAIN
        return pltpu.make_async_remote_copy(
            src_ref=src.at[rows_of(j, a)], dst_ref=dst_of(a, j), send_sem=send.at[a, i - 1], recv_sem=recv.at[a, i - 1],
            device_id=chain_peer(i)[1], device_id_type=MESH)

    def tok_slot(a, j):
        return xin.at[a, j]

    def cot_slot(a, j):
        return up.at[LAYERS - 1, a, j]

    def own_tok(a):
        return pltpu.make_async_copy(tok.at[rows_of(k, a)], xin.at[a, k], own_sem.at[a])

    def own_cot(a):
        return pltpu.make_async_copy(cot.at[rows_of(k, a)], up.at[LAYERS - 1, a, k], own_sem.at[PARTS + a])

    def own_out(a):
        return pltpu.make_async_copy(ready.at[a, k], out.at[rows_of(k, a)], own_sem.at[2 * PARTS + a])

    def give_back(a, i):
        j, peer = chain_peer(i)
        return pltpu.make_async_remote_copy(
            src_ref=ready.at[a, j], dst_ref=out.at[rows_of(k, a)], send_sem=out_send.at[a, i - 1],
            recv_sem=out_recv.at[a, i - 1], device_id=peer, device_id_type=MESH)

    def given_back(a, i):
        j = (k + CHAIN - i) % CHAIN
        return pltpu.make_async_remote_copy(
            src_ref=ready.at[a, j], dst_ref=out.at[rows_of(j, a)], send_sem=out_send.at[a, i - 1],
            recv_sem=out_recv.at[a, i - 1], device_id=chain_peer(i)[1], device_id_type=MESH)

    for a in range(PARTS):
        @pl.loop(0, CHAIN - 1)
        def _(t):
            deal(tok, tok_slot, tok_send, tok_recv, a, crossing_first(t)).start()

        own_tok(a).start()
    def send_cot(a):
        for i in (1, 3, 5):
            if a == 0:
                deal(tok, tok_slot, tok_send, tok_recv, 0, i).wait_send()
            else:
                deal(cot, cot_slot, cot_send, cot_recv, 0, i).wait_send()

        @pl.loop(0, CHAIN - 1)
        def _(t):
            deal(cot, cot_slot, cot_send, cot_recv, a, crossing_first(t)).start()

        own_cot(a).start()

    def round_signal(t):
        pl.semaphore_signal(round_sem.at[t, 0], inc=1, device_id=above, device_id_type=MESH)
        pl.semaphore_signal(round_sem.at[t, 1], inc=1, device_id=below, device_id_type=MESH)

    def round_wait(t):
        pl.semaphore_wait(round_sem.at[t, 0], 1)
        pl.semaphore_wait(round_sem.at[t, 1], 1)

    @pl.loop(0, 3)
    def _(t):
        round_signal(t)
        round_wait(t)

    round_signal(3)

    def between_layers(n):
        @pl.when(n < 5)
        def _():
            round_wait(3 + n)

        @pl.when(n < 4)
        def _():
            round_signal(4 + n)

        @pl.when(n == 3)
        def _():
            send_cot(1)

        @pl.when(n == 4)
        def _():
            pl.semaphore_signal(pair_sem, inc=1, device_id=(seq, dp + 1 - 2 * core), device_id_type=MESH)

        @pl.when(n == 5)
        def _():
            pl.semaphore_wait(pair_sem, 1)

    zeros = jnp.zeros((4, ROWS, C), BF16)
    for layer in range(LAYERS):
        for a in range(PARTS):
            normed[layer, a, 0:4] = zeros
            normed[layer, a, 12:16] = zeros
    grad_hid[0:4] = zeros
    grad_hid[12:16] = zeros
    taps_acc[...] = jnp.zeros_like(taps_acc)
    taps_part[...] = jnp.zeros_like(taps_part)
    load_taps.wait()

    pair = (seq, dp + 1 - 2 * core)

    def give_active(layer, a):
        return pltpu.make_async_remote_copy(
            src_ref=active.at[layer, a], dst_ref=sib_active.at[layer, a], send_sem=act_sem.at[layer, a, 0],
            recv_sem=act_sem.at[layer, a, 1], device_id=pair, device_id_type=MESH)

    def give_up(layer, a):
        return pltpu.make_async_remote_copy(
            src_ref=up.at[layer, a, :, :, pl.ds(pl.multiple_of((1 - core) * HALF, HALF), HALF)],
            dst_ref=sib_up.at[layer, a], send_sem=up_sem.at[layer, a, 0], recv_sem=up_sem.at[layer, a, 1],
            device_id=pair, device_id_type=MESH)

    def shift_of(layer):
        return 1 + layer + layer * (layer - 1) // 2

    def block_of_columns(n):
        return pl.ds(pl.multiple_of(n * COLS, COLS), COLS)

    def forward(a, layer):
        shift = shift_of(layer)

        @pl.loop(0, CHAIN, unroll=2)
        def _(j):
            value = xin[a, j].astype(F32)
            mean = jnp.sum(value * value, axis=-1, keepdims=True) * (1.0 / C)
            inv = lax.rsqrt(mean + EPSILON)
            value = value * inv
            inverse[layer, a, j] = jnp.broadcast_to(inv, (ROWS, 128))
            normal[layer, a, j] = value
            normed[layer, a, 4 + j] = value.astype(BF16)

        @pl.loop(0, CHAIN, unroll=2)
        def _(j):
            hid = (
                taps[layer, 0:1, :] * normed[layer, a, 4 + j - shift].astype(F32)
                + taps[layer, 1:2, :] * normed[layer, a, 4 + j].astype(F32)
                + taps[layer, 2:3, :] * normed[layer, a, 4 + j + shift].astype(F32)
            )
            square = hid * hid
            tanh = jnp.tanh(GELU_A * hid * (1.0 + GELU_B * square))
            half = 0.5 * (1.0 + tanh)
            active[layer, a, j] = (hid * half).astype(BF16)
            slope[layer, a, j] = half + (0.5 * GELU_A) * hid * (1.0 - tanh * tanh) * (1.0 + (3.0 * GELU_B) * square)

        give_active(layer, a).start()
        between_layers(a * LAYERS + layer)

        @pl.when(a == 0)
        def _():
            load(layer).wait()

        @pl.when(layer < LAYERS - 1)
        def _():
            @pl.loop(0, C // COLS)
            def _(n):
                cols = block_of_columns(n)
                product = jnp.dot(active[layer, a].reshape(CHAIN * ROWS, C), w[layer, :, cols], preferred_element_type=F32)
                xin[a, :, :, cols] = (
                    xin[a, :, :, cols].astype(F32) + product.reshape(CHAIN, ROWS, COLS)).astype(BF16)

    def backward(a, layer):
        shift = shift_of(layer)

        @pl.loop(0, C // COLS)
        def _(n):
            cols = block_of_columns(n)
            spread = lax.dot_general(
                up[layer, a].reshape(CHAIN * ROWS, C), w[layer, cols, :], (((1,), (1,)), ((), ())),
                preferred_element_type=F32)
            grad_hid[4:12, :, cols] = (spread.reshape(CHAIN, ROWS, COLS) * slope[layer, a, :, :, cols]).astype(BF16)

        @pl.when(layer == LAYERS - 1)
        def _():
            grad[...] = up[layer, a].astype(F32)

        @pl.loop(0, CHAIN, unroll=2)
        def _(j):
            mid = grad_hid[4 + j].astype(F32)
            for t in range(3):
                term = mid * normed[layer, a, 4 + j + (t - 1) * shift].astype(F32)
                taps_acc[layer, t] += term[0:8] + term[8:16]
            moved = (
                taps[layer, 1:2, :] * mid
                + taps[layer, 0:1, :] * grad_hid[4 + j + shift].astype(F32)
                + taps[layer, 2:3, :] * grad_hid[4 + j - shift].astype(F32)
            )
            value = normal[layer, a, j]
            mean = jnp.sum(moved * value, axis=-1, keepdims=True) * (1.0 / C)
            after = grad[j] + inverse[layer, a, j, :, 0:1] * (moved - value * mean)
            grad[j] = after
            ready[a, j] = after.astype(BF16)

            @pl.when(layer > 0)
            def _():
                up[layer - 1, a, j] = after.astype(BF16)

    def point_terms(layer):
        for a in range(PARTS):
            give_active(layer, a).wait_recv()
            give_up(layer, a).wait_recv()
        mine = up[layer, :, :, :, pl.ds(pl.multiple_of(core * HALF, HALF), HALF)].reshape(SLAB, HALF)
        rows = jnp.concatenate([mine, sib_up[layer].reshape(SLAB, HALF)], axis=0)
        over_rows = (((0,), (0,)), ((), ()))

        def acts(m):
            cols = slice(m * HALF, (m + 1) * HALF)
            return jnp.concatenate(
                [active[layer, :, :, :, cols].reshape(SLAB, HALF), sib_active[layer, :, :, :, cols].reshape(SLAB, HALF)],
                axis=0)

        @pl.when(core == 0)
        def _():
            for m in range(2):
                product = lax.dot_general(rows, acts(m), over_rows, preferred_element_type=F32)
                summed[layer, :, m] = product.astype(BF16).reshape(4, PIECE, HALF)

        @pl.when(core == 1)
        def _():
            for m in range(2):
                product = lax.dot_general(acts(m), rows, over_rows, preferred_element_type=F32)
                summed[layer, 2 * m:2 * m + 2] = product.astype(BF16).reshape(2, 2, PIECE, HALF)

        for n in range(4):
            around(layer, n).start()

    def tap_terms():
        for layer in range(LAYERS):
            for t in range(3):
                line = jnp.sum(taps_acc[layer, t], axis=0, keepdims=True)
                for b in range(C // 128):
                    row = (layer * 3 + t) * (C // 128) + b
                    taps_part[row // 7, row % 7:row % 7 + 1, :] = line[:, b * 128:(b + 1) * 128]

    def around(layer, n):
        way = n % 2
        place = (p + 1 + 2 * way) % 4
        if n < 2:
            src, dst = summed.at[layer, (p + 2) % 4, way], half_way.at[layer, way]
        else:
            half = 1 - way if n < 4 else way
            src, dst = summed.at[layer, place, half], from_a.at[layer, way, half]
        return pltpu.make_async_remote_copy(
            src_ref=src, dst_ref=dst, send_sem=a_send.at[layer, n], recv_sem=a_recv.at[layer, n],
            device_id=first_peer(place), device_id_type=MESH)

    def parcel(layer, i):
        place, peer = second_peer(i)
        return pltpu.make_async_remote_copy(
            src_ref=to_b.at[layer, place], dst_ref=from_b.at[layer, i - 1], send_sem=red_send.at[layer, i - 1],
            recv_sem=red_recv.at[layer, i - 1], device_id=peer, device_id_type=MESH)

    def to_owner(e):
        place = e // 2
        return pltpu.make_async_remote_copy(
            src_ref=to_z.at[e % 2, place], dst_ref=from_z.at[z], send_sem=z_send.at[e],
            recv_sem=z_recv.at[z], device_id=z_device(core * 8 + place, e % 2), device_id_type=MESH)

    def z_arrival(m):
        return pltpu.make_async_remote_copy(
            src_ref=to_z.at[0, 0], dst_ref=from_z.at[m], send_sem=z_send.at[m],
            recv_sem=z_recv.at[m], device_id=z_device(m, zh), device_id_type=MESH)

    def is_own(e):
        return jnp.logical_and(core == zh, e == (h * 4 + c) * 2 + core)

    def step_ring(layer):
        for way in range(2):
            around(layer, way).wait_recv()
            place = (p + 1 + 2 * way) % 4
            summed[layer, place, way] = (
                summed[layer, place, way].astype(F32) + half_way[layer, way].astype(F32)).astype(BF16)
            around(layer, 4 + way).start()

    def step_first(layer):
        for n in range(2, 6):
            around(layer, n).wait_recv()

        @pl.when(core == 0)
        def _():
            for half in range(2):
                for b in range(HALF // 128):
                    lanes = slice(b * 128, (b + 1) * 128)
                    total = (
                        summed[layer, p, half, :, lanes].astype(F32) + from_a[layer, 0, half, :, lanes].astype(F32)
                        + from_a[layer, 1, half, :, lanes].astype(F32))
                    total = jnp.concatenate([total, jnp.zeros((128 - PIECE, 128), F32)], axis=0)
                    first = half * HALF + b * 128
                    for row in range(first, first + 128, 64):
                        to_b[layer, row // 192, row % 192:row % 192 + 64, :] = total.T[row - first:row - first + 64].astype(BF16)

        @pl.when(core == 1)
        def _():
            for half in range(2):
                total = (
                    summed[layer, p, half].astype(F32) + from_a[layer, 0, half].astype(F32)
                    + from_a[layer, 1, half].astype(F32))
                for place in range(4):
                    value = total[:, place * PIECE:(place + 1) * PIECE]
                    value = jnp.concatenate([value, jnp.zeros((PIECE, 128 - PIECE), F32)], axis=1)
                    to_b[layer, place, half * PIECE:(half + 1) * PIECE, :] = value.astype(BF16)

        for i in range(1, 4):
            parcel(layer, i).start()

    def step_second():
        totals = []
        for layer in range(LAYERS):
            for i in range(1, 4):
                parcel(layer, i).wait_recv()
            total = to_b[layer, r].astype(F32)
            for i in range(3):
                total = total + from_b[layer, i].astype(F32)
            totals.append(total)
        for of_core in range(2):
            first = of_core * 48
            top = jnp.concatenate(
                [totals[2][:, first:first + 48], totals[1][:, first:first + 48], totals[0][:, first:first + 32]], axis=1)
            rest = totals[0][:, first + 32:first + 48].reshape(8, 3, 8, 16)
            rest = [rest[:, g].reshape(64, 16) for g in range(3)] + [jnp.zeros((64, 80), F32)]
            rest = jnp.concatenate(rest, axis=1)
            whole = jnp.concatenate([top.reshape(8, 24, 128), rest.reshape(8, 8, 128)], axis=1)
            to_z[of_core] = whole.astype(BF16)

        @pl.loop(0, 16)
        def _(e):
            @pl.when(is_own(e))
            def _():
                from_z[z] = to_z[core, h * 4 + c]

            @pl.when(jnp.logical_not(is_own(e)))
            def _():
                to_owner(e).start()

    def step_last():
        @pl.loop(0, 16)
        def _(m):
            @pl.when(jnp.logical_not(jnp.logical_and(core == zh, z == m)))
            def _():
                z_arrival(m).wait_recv()

        total = from_z[0].astype(F32)
        for m in range(1, 16):
            total = total + from_z[m].astype(F32)
        total = total * factor
        out_point[2] = total[0:24, 0:48]
        out_point[1] = total[0:24, 48:96]
        rest = jnp.concatenate([total[24:32, g * 16:(g + 1) * 16] for g in range(3)], axis=0)
        out_point[0] = jnp.concatenate([total[0:24, 96:128], rest], axis=1)

    tap_partners = (range(1, 8), range(1, 4), range(1, 16), range(1, 8))

    def tap_copy(step, i):
        place, peer = tap_peer(step, i)
        if step == 0:
            src, dst = taps_part.at[place], taps_in.at[0, i - 1]
        elif step == 3:
            src, dst = taps_one.at[2], taps_all.at[dp % 8]
        else:
            src, dst = taps_one.at[step - 1], taps_in.at[step, i - 1]
        return pltpu.make_async_remote_copy(
            src_ref=src, dst_ref=dst, send_sem=tap_send.at[step, i - 1], recv_sem=tap_recv.at[step, i - 1],
            device_id=peer, device_id_type=MESH)

    def tap_gathered(i):
        place = (dp % 8 + 8 - i) % 8
        return pltpu.make_async_remote_copy(
            src_ref=taps_one.at[2], dst_ref=taps_all.at[place], send_sem=tap_send.at[3, i - 1],
            recv_sem=tap_recv.at[3, i - 1], device_id=tap_peer(3, i)[1], device_id_type=MESH)

    def tap_start(step):
        @pl.loop(tap_partners[step].start, tap_partners[step].stop)
        def _(i):
            tap_copy(step, i).start()

    def tap_step(step):
        @pl.loop(tap_partners[step].start, tap_partners[step].stop)
        def _(i):
            tap_copy(step, i).wait_recv()

        total = taps_part[dp % 8] if step == 0 else taps_one[step - 1]
        for i in tap_partners[step]:
            total = total + taps_in[step, i - 1]
        taps_one[step] = total
        if step == 2:
            taps_all[dp % 8] = total
        tap_start(step + 1)

    def tap_last():
        @pl.loop(1, 8)
        def _(i):
            tap_gathered(i).wait_recv()

        for layer in range(LAYERS):
            for t in range(3):
                for b in range(C // 128):
                    row = (layer * 3 + t) * (C // 128) + b
                    out_taps[layer, t:t + 1, b * 128:(b + 1) * 128] = taps_all[row // 7, row % 7:row % 7 + 1, :] * factor

    def wait_dealt(src, slot, sends, recvs, own, a):
        @pl.loop(1, CHAIN)
        def _(i):
            dealt(src, slot, sends, recvs, a, i).wait_recv()

        own(a).wait()

    def send_back(a):
        @pl.loop(0, CHAIN - 1)
        def _(t):
            give_back(a, crossing_first(t)).start()

        own_out(a).start()

    send_cot(0)

    @pl.loop(0, PARTS * LAYERS)
    def _(n):
        a, layer = n // LAYERS, n % LAYERS

        @pl.when(layer == 0)
        def _():
            wait_dealt(tok, tok_slot, tok_send, tok_recv, own_tok, a)

        forward(a, layer)

    @pl.loop(0, PARTS * LAYERS)
    def _(n):
        a, layer = n // LAYERS, LAYERS - 1 - n % LAYERS

        @pl.when(layer == LAYERS - 1)
        def _():
            wait_dealt(cot, cot_slot, cot_send, cot_recv, own_cot, a)
            give_up(layer, a).start()

        backward(a, layer)

        @pl.when(layer > 0)
        def _():
            give_up(layer - 1, a).start()

        @pl.when(layer == 0)
        def _():
            send_back(a)

        @pl.when(a == PARTS - 1)
        def _():
            @pl.when(layer < LAYERS - 1)
            def _():
                step_ring(layer + 1)

            point_terms(layer)

    tap_terms()
    tap_start(0)

    @pl.loop(0, LAYERS)
    def _(n):
        @pl.when(n == 1)
        def _():
            step_ring(0)
            tap_step(0)

        @pl.when(n == 2)
        def _():
            tap_step(1)

        step_first(LAYERS - 1 - n)

    step_second()

    for a in range(PARTS):
        own_out(a).wait()

    @pl.loop(1, CHAIN)
    def _(i):
        for a in range(PARTS):
            give_back(a, i).wait_send()
        deal(cot, cot_slot, cot_send, cot_recv, PARTS - 1, i).wait_send()

    for i in range(1, CHAIN):
        deal(tok, tok_slot, tok_send, tok_recv, 1, i).wait_send()
    for i in (2, 4, 6, 7):
        deal(tok, tok_slot, tok_send, tok_recv, 0, i).wait_send()
        deal(cot, cot_slot, cot_send, cot_recv, 0, i).wait_send()
    @pl.loop(0, LAYERS)
    def _(layer):
        for a in range(PARTS):
            give_active(layer, a).wait_send()
            give_up(layer, a).wait_send()
        for n in range(6):
            around(layer, n).wait_send()
        for i in range(1, 4):
            parcel(layer, i).wait_send()
    for step in range(2):
        @pl.loop(tap_partners[step].start, tap_partners[step].stop)
        def _(i):
            tap_copy(step, i).wait_send()

    tap_step(2)
    for a in range(PARTS):
        @pl.loop(1, CHAIN)
        def _(i):
            given_back(a, i).wait_recv()

    @pl.loop(0, 16)
    def _(e):
        @pl.when(jnp.logical_not(is_own(e)))
        def _():
            to_owner(e).wait_send()

    @pl.loop(tap_partners[2].start, tap_partners[2].stop)
    def _(i):
        tap_copy(2, i).wait_send()

    step_last()
    tap_last()

    @pl.loop(tap_partners[3].start, tap_partners[3].stop)
    def _(i):
        tap_copy(3, i).wait_send()


def local(factor, tokens, cotangent, conv_kernel, point_weight):
    any_space = pl.BlockSpec(memory_space=pl.ANY)
    vmem = pl.BlockSpec(memory_space=pltpu.VMEM)
    part = (PARTS, CHAIN, ROWS, C)
    scratch = [
        pltpu.VMEM(part, BF16),
        pltpu.VMEM((LAYERS, PARTS, CHAIN + 8, ROWS, C), BF16),
        pltpu.VMEM((LAYERS,) + part, F32),
        pltpu.VMEM((LAYERS, PARTS, CHAIN, ROWS, 128), F32),
        pltpu.VMEM((LAYERS,) + part, F32),
        pltpu.VMEM((LAYERS,) + part, BF16),
        pltpu.VMEM((LAYERS,) + part, BF16),
        pltpu.VMEM((CHAIN, ROWS, C), F32),
        pltpu.VMEM((CHAIN + 8, ROWS, C), BF16),
        pltpu.VMEM(part, BF16),
        pltpu.VMEM((LAYERS, C, C), BF16),
        pltpu.VMEM((LAYERS, 3, C), F32),
        pltpu.VMEM((LAYERS,) + part, BF16),
        pltpu.VMEM((LAYERS, PARTS, CHAIN, ROWS, HALF), BF16),
        pltpu.VMEM((LAYERS, 4, 2, PIECE, HALF), BF16),
        pltpu.VMEM((LAYERS, 2, PIECE, HALF), BF16),
        pltpu.VMEM((LAYERS, 2, 2, PIECE, HALF), BF16),
        pltpu.VMEM((LAYERS, 4, 192, 128), BF16),
        pltpu.VMEM((LAYERS, 3, 192, 128), BF16),
        pltpu.VMEM((2, 8, 32, 128), BF16),
        pltpu.VMEM((16, 32, 128), BF16),
        pltpu.VMEM((LAYERS, 3, 8, C), F32),
        pltpu.VMEM((8, 8, 128), F32),
        pltpu.VMEM((3, 8, 128), F32),
        pltpu.VMEM((3, 15, 8, 128), F32),
        pltpu.VMEM((8, 8, 128), F32),
        pltpu.SemaphoreType.DMA((PARTS, CHAIN - 1)),
        pltpu.SemaphoreType.DMA((PARTS, CHAIN - 1)),
        pltpu.SemaphoreType.DMA((PARTS, CHAIN - 1)),
        pltpu.SemaphoreType.DMA((PARTS, CHAIN - 1)),
        pltpu.SemaphoreType.DMA((PARTS, CHAIN - 1)),
        pltpu.SemaphoreType.DMA((PARTS, CHAIN - 1)),
        pltpu.SemaphoreType.DMA((3 * PARTS,)),
        pltpu.SemaphoreType.DMA((LAYERS + 1,)),
        pltpu.SemaphoreType.DMA((LAYERS, PARTS, 2)),
        pltpu.SemaphoreType.DMA((LAYERS, PARTS, 2)),
        pltpu.SemaphoreType.DMA((LAYERS, 6)),
        pltpu.SemaphoreType.DMA((LAYERS, 6)),
        pltpu.SemaphoreType.DMA((LAYERS, 3)),
        pltpu.SemaphoreType.DMA((LAYERS, 3)),
        pltpu.SemaphoreType.DMA((16,)),
        pltpu.SemaphoreType.DMA((16,)),
        pltpu.SemaphoreType.DMA((4, 15)),
        pltpu.SemaphoreType.DMA((4, 15)),
        pltpu.SemaphoreType.REGULAR((8, 2)),
        pltpu.SemaphoreType.REGULAR,
    ]
    out, out_point, out_taps = pl.pallas_call(
        functools.partial(kernel, factor),
        out_shape=(
            pltpu.VMEM((SLAB, C), BF16),
            pltpu.VMEM((LAYERS, 24, 48), F32),
            pltpu.VMEM((LAYERS, 3, C), F32),
        ),
        in_specs=[any_space] * 4,
        out_specs=(any_space, vmem, vmem),
        scratch_shapes=scratch,
        compiler_params=pltpu.CompilerParams(collective_id=0, has_side_effects=True, vmem_limit_bytes=60 * 2**20),
        cost_estimate=pl.CostEstimate(flops=2 * 9 * SLAB * C * C, bytes_accessed=6 * 2**20, transcendentals=LAYERS * SLAB * C),
    )(tokens[0], cotangent[0], conv_kernel, point_weight)
    return out[None], out_point, out_taps


def solution(mesh):
    factor = 1.0 / math.sqrt(mesh.shape["seq"] * mesh.shape["dp"] * SLAB)
    P = jax.sharding.PartitionSpec
    return jax.shard_map(
        functools.partial(local, factor),
        mesh=mesh,
        in_specs=(P("dp", "seq", None), P("dp", "seq", None), P(), P()),
        out_specs=(P("dp", "seq", None), P(None, "seq", "dp"), P()),
        check_vma=False,
    )
```

```python
import functools
import math

import jax
import jax.numpy as jnp
from jax import lax
from jax.experimental import pallas as pl
from jax.experimental.pallas import tpu as pltpu

EPSILON = 1e-06
MESH = pl.DeviceIdType.MESH
F32 = jnp.float32
BF16 = jnp.bfloat16

C = 768
LAYERS = 3
CHAIN = 8
ROWS = 16
PARTS = 2
SLAB = 256
COLS = 256
HALF = C // 2
PIECE = 96
GELU_A = math.sqrt(2.0 / math.pi)
GELU_B = 0.044715


def div(a, b):
    return lax.div(a, jnp.int32(b))


def rem(a, b):
    return lax.rem(a, jnp.int32(b))


def kernel(factor, tok, cot, taps_hbm, weight, out, out_point, out_taps, *scratch):
    (xin, normed, normal, inverse, slope, active, up, grad, grad_hid, ready, w, taps, sib_active, sib_up, summed, half_way, from_a,
     to_b, from_b, to_z, from_z, taps_acc, taps_part, taps_one, taps_in, taps_all,
     tok_send, tok_recv, cot_send, cot_recv, out_send, out_recv, own_sem, w_sem, act_sem, up_sem, a_send, a_recv, red_send, red_recv,
     z_send, z_recv, tap_send, tap_recv, round_sem, pair_sem) = scratch
    seq = lax.axis_index("seq")
    dp = lax.axis_index("dp")
    k, c = div(seq, 4), rem(seq, 4)
    y, h = div(seq, 8), rem(k, 2)
    zh, core = div(dp, 8), rem(dp, 2)
    eighth = dp - zh * 8
    x = div(eighth, 2)
    block = zh * 2 + h
    p = x + core * (y - x)
    r = y + core * (x - y)

    def chain_peer(i):
        j = rem(k + i, CHAIN)
        return j, (j * 4 + c, dp)

    def first_peer(place):
        return seq + core * (place - y) * 8, dp + (1 - core) * (place - x) * 2

    def second_peer(i):
        place = rem(r + i, 4)
        return place, (seq + (1 - core) * (place - y) * 8, dp + core * (place - x) * 2)

    z = zh * 8 + h * 4 + c

    def z_device(place, of_core):
        half = div(place, 8)
        return y * 8 + place - half * 8, half * 8 + x * 2 + of_core

    def tap_peer(step, i):
        if step in (0, 3):
            place = rem(eighth + i, 8)
            return place, (seq, zh * 8 + place)
        if step == 1:
            place = rem(y + i, 4)
            return place, (place * 8 + h * 4 + c, dp)
        place = rem(z + i, 16)
        return place, z_device(place, core)

    barrier = pltpu.get_barrier_semaphore()

    def greet(peer):
        pl.semaphore_signal(barrier, inc=1, device_id=peer, device_id_type=MESH)

    @pl.loop(1, CHAIN)
    def _(i):
        greet(chain_peer(i)[1])
        greet(tap_peer(0, i)[1])

    above, below = z_device(rem(z + 1, 16), core), z_device(rem(z + 15, 16), core)
    greet(above)
    greet(below)

    def load(layer):
        return pltpu.make_async_copy(weight.at[layer], w.at[layer], w_sem.at[layer])

    load_taps = pltpu.make_async_copy(taps_hbm, taps, w_sem.at[LAYERS])
    load_taps.start()
    for layer in range(LAYERS):
        load(layer).start()

    pl.semaphore_wait(barrier, 16)

    def crossing_first(t):
        return 2 * t + 1 - 7 * div(t, 4)

    def deal_tok(a, i, arriving=False):
        j, peer = chain_peer(i)
        slot = rem(k + CHAIN - i, CHAIN) if arriving else k
        return pltpu.make_async_remote_copy(
            src_ref=tok.at[j, a], dst_ref=xin.at[a, slot], send_sem=tok_send.at[a, i - 1],
            recv_sem=tok_recv.at[a, i - 1], device_id=peer, device_id_type=MESH)

    def deal_cot(a, i, arriving=False):
        j, peer = chain_peer(i)
        slot = rem(k + CHAIN - i, CHAIN) if arriving else k
        return pltpu.make_async_remote_copy(
            src_ref=cot.at[j, a], dst_ref=up.at[LAYERS - 1, a, slot], send_sem=cot_send.at[a, i - 1],
            recv_sem=cot_recv.at[a, i - 1], device_id=peer, device_id_type=MESH)

    def own_tok(a):
        return pltpu.make_async_copy(tok.at[k, a], xin.at[a, k], own_sem.at[2 * PARTS + a])

    def own_cot(a):
        return pltpu.make_async_copy(cot.at[k, a], up.at[LAYERS - 1, a, k], own_sem.at[PARTS + a])

    def own_out(a):
        return pltpu.make_async_copy(ready.at[a, k], out.at[k, a], own_sem.at[a])

    def give_back(a, i):
        j, peer = chain_peer(i)
        return pltpu.make_async_remote_copy(
            src_ref=ready.at[a, j], dst_ref=out.at[k, a], send_sem=out_send.at[a, i - 1],
            recv_sem=out_recv.at[a, i - 1], device_id=peer, device_id_type=MESH)

    def given_back(a, i):
        j = rem(k + CHAIN - i, CHAIN)
        return pltpu.make_async_remote_copy(
            src_ref=ready.at[a, j], dst_ref=out.at[j, a], send_sem=out_send.at[a, i - 1],
            recv_sem=out_recv.at[a, i - 1], device_id=chain_peer(i)[1], device_id_type=MESH)

    @pl.loop(0, PARTS)
    def _(a):
        @pl.loop(0, CHAIN - 1)
        def _(t):
            deal_tok(a, crossing_first(t)).start()

        own_tok(a).start()

    def send_cot(a):
        for i in (1, 3, 5):
            if a == 0:
                deal_tok(0, i).wait_send()
            else:
                deal_cot(0, i).wait_send()

        @pl.loop(0, CHAIN - 1)
        def _(t):
            deal_cot(a, crossing_first(t)).start()

        own_cot(a).start()

    def round_signal(t):
        pl.semaphore_signal(round_sem.at[t, 0], inc=1, device_id=above, device_id_type=MESH)
        pl.semaphore_signal(round_sem.at[t, 1], inc=1, device_id=below, device_id_type=MESH)

    def round_wait(t):
        pl.semaphore_wait(round_sem.at[t, 0], 1)
        pl.semaphore_wait(round_sem.at[t, 1], 1)

    @pl.loop(0, 3)
    def _(t):
        round_signal(t)
        round_wait(t)

    round_signal(3)

    def between_layers(n):
        @pl.when(n < 5)
        def _():
            round_wait(3 + n)

        @pl.when(n < 4)
        def _():
            round_signal(4 + n)

        @pl.when(n == 3)
        def _():
            send_cot(1)

        @pl.when(n == 4)
        def _():
            pl.semaphore_signal(pair_sem, inc=1, device_id=(seq, dp + 1 - 2 * core), device_id_type=MESH)

        @pl.when(n == 5)
        def _():
            pl.semaphore_wait(pair_sem, 1)

    zeros = jnp.zeros((4, ROWS, C), BF16)
    for layer in range(LAYERS):
        for a in range(PARTS):
            normed[layer, a, 0:4] = zeros
            normed[layer, a, 12:16] = zeros
    grad_hid[0:4] = zeros
    grad_hid[12:16] = zeros
    taps_acc[...] = jnp.zeros_like(taps_acc)
    taps_part[...] = jnp.zeros_like(taps_part)
    load_taps.wait()

    pair = (seq, dp + 1 - 2 * core)

    def give_active(layer, a):
        return pltpu.make_async_remote_copy(
            src_ref=active.at[layer, a], dst_ref=sib_active.at[layer, a], send_sem=act_sem.at[layer, a, 0],
            recv_sem=act_sem.at[layer, a, 1], device_id=pair, device_id_type=MESH)

    def give_up(layer, a):
        return pltpu.make_async_remote_copy(
            src_ref=up.at[layer, a, :, :, pl.ds(pl.multiple_of((1 - core) * HALF, HALF), HALF)],
            dst_ref=sib_up.at[layer, a], send_sem=up_sem.at[layer, a, 0], recv_sem=up_sem.at[layer, a, 1],
            device_id=pair, device_id_type=MESH)

    def shift_of(layer):
        return 1 + layer + div(layer * (layer - 1), 2)

    def block_of_columns(n):
        return pl.ds(pl.multiple_of(n * COLS, COLS), COLS)

    def forward(a, layer):
        shift = shift_of(layer)

        @pl.loop(0, CHAIN, unroll=8)
        def _(j):
            value = xin[a, j].astype(F32)
            mean = jnp.sum(value * value, axis=-1, keepdims=True) * (1.0 / C)
            inv = lax.rsqrt(mean + EPSILON)
            value = value * inv
            inverse[layer, a, j] = jnp.broadcast_to(inv, (ROWS, 128))
            normal[layer, a, j] = value
            normed[layer, a, 4 + j] = value.astype(BF16)

        @pl.loop(0, CHAIN, unroll=8)
        def _(j):
            hid = (
                taps[layer, 0:1, :] * normed[layer, a, 4 + j - shift].astype(F32)
                + taps[layer, 1:2, :] * normed[layer, a, 4 + j].astype(F32)
                + taps[layer, 2:3, :] * normed[layer, a, 4 + j + shift].astype(F32)
            )
            square = hid * hid
            tanh = jnp.tanh(GELU_A * hid * (1.0 + GELU_B * square))
            half = 0.5 * (1.0 + tanh)
            active[layer, a, j] = (hid * half).astype(BF16)
            slope[layer, a, j] = half + (0.5 * GELU_A) * hid * (1.0 - tanh * tanh) * (1.0 + (3.0 * GELU_B) * square)

        give_active(layer, a).start()
        between_layers(a * LAYERS + layer)

        @pl.when(a == 0)
        def _():
            load(layer).wait()

        @pl.when(layer < LAYERS - 1)
        def _():
            @pl.loop(0, C // COLS)
            def _(n):
                cols = block_of_columns(n)
                product = jnp.dot(active[layer, a].reshape(CHAIN * ROWS, C), w[layer, :, cols], preferred_element_type=F32)
                xin[a, :, :, cols] = (
                    xin[a, :, :, cols].astype(F32) + product.reshape(CHAIN, ROWS, COLS)).astype(BF16)

    def backward(a, layer):
        shift = shift_of(layer)

        @pl.loop(0, C // COLS)
        def _(n):
            cols = block_of_columns(n)
            spread = lax.dot_general(
                up[layer, a].reshape(CHAIN * ROWS, C), w[layer, cols, :], (((1,), (1,)), ((), ())),
                preferred_element_type=F32)
            grad_hid[4:12, :, cols] = (spread.reshape(CHAIN, ROWS, COLS) * slope[layer, a, :, :, cols]).astype(BF16)

        @pl.when(layer == LAYERS - 1)
        def _():
            grad[...] = up[layer, a].astype(F32)

        @pl.loop(0, CHAIN, unroll=8)
        def _(j):
            mid = grad_hid[4 + j].astype(F32)
            for t in range(3):
                term = mid * normed[layer, a, 4 + j + (t - 1) * shift].astype(F32)
                taps_acc[layer, t] += term[0:8] + term[8:16]
            moved = (
                taps[layer, 1:2, :] * mid
                + taps[layer, 0:1, :] * grad_hid[4 + j + shift].astype(F32)
                + taps[layer, 2:3, :] * grad_hid[4 + j - shift].astype(F32)
            )
            value = normal[layer, a, j]
            mean = jnp.sum(moved * value, axis=-1, keepdims=True) * (1.0 / C)
            after = grad[j] + inverse[layer, a, j, :, 0:1] * (moved - value * mean)
            grad[j] = after
            ready[a, j] = after.astype(BF16)

            @pl.when(layer > 0)
            def _():
                up[layer - 1, a, j] = after.astype(BF16)

    def point_terms(layer):
        for a in range(PARTS):
            give_active(layer, a).wait_recv()
            give_up(layer, a).wait_recv()
        mine = up[layer, :, :, :, pl.ds(pl.multiple_of(core * HALF, HALF), HALF)].reshape(SLAB, HALF)
        rows = jnp.concatenate([mine, sib_up[layer].reshape(SLAB, HALF)], axis=0)
        over_rows = (((0,), (0,)), ((), ()))

        def acts(m):
            cols = slice(m * HALF, (m + 1) * HALF)
            return jnp.concatenate(
                [active[layer, :, :, :, cols].reshape(SLAB, HALF), sib_active[layer, :, :, :, cols].reshape(SLAB, HALF)],
                axis=0)

        @pl.when(core == 0)
        def _():
            for m in range(2):
                product = lax.dot_general(rows, acts(m), over_rows, preferred_element_type=F32)
                summed[layer, :, m] = product.astype(BF16).reshape(4, PIECE, HALF)

        @pl.when(core == 1)
        def _():
            for m in range(2):
                product = lax.dot_general(acts(m), rows, over_rows, preferred_element_type=F32)
                summed[layer, 2 * m:2 * m + 2] = product.astype(BF16).reshape(2, 2, PIECE, HALF)

        for n in range(4):
            around(layer, n).start()

    def tap_terms():
        for layer in range(LAYERS):
            for t in range(3):
                line = jnp.sum(taps_acc[layer, t], axis=0, keepdims=True)
                for b in range(C // 128):
                    row = (layer * 3 + t) * (C // 128) + b
                    taps_part[row // 7, row % 7:row % 7 + 1, :] = line[:, b * 128:(b + 1) * 128]

    def around(layer, n):
        way = n % 2
        place = rem(p + 1 + 2 * way, 4)
        if n < 2:
            src, dst = summed.at[layer, rem(p + 2, 4), way], half_way.at[layer, way]
        else:
            half = 1 - way if n < 4 else way
            src, dst = summed.at[layer, place, half], from_a.at[layer, way, half]
        return pltpu.make_async_remote_copy(
            src_ref=src, dst_ref=dst, send_sem=a_send.at[layer, n], recv_sem=a_recv.at[layer, n],
            device_id=first_peer(place), device_id_type=MESH)

    def parcel(layer, i):
        place, peer = second_peer(i)
        return pltpu.make_async_remote_copy(
            src_ref=to_b.at[layer, place], dst_ref=from_b.at[layer, i - 1], send_sem=red_send.at[layer, i - 1],
            recv_sem=red_recv.at[layer, i - 1], device_id=peer, device_id_type=MESH)

    def to_owner(e):
        place = div(e, 2)
        of_core = e - place * 2
        return pltpu.make_async_remote_copy(
            src_ref=to_z.at[of_core, place], dst_ref=from_z.at[z], send_sem=z_send.at[e],
            recv_sem=z_recv.at[z], device_id=z_device(core * 8 + place, of_core), device_id_type=MESH)

    def z_arrival(m):
        return pltpu.make_async_remote_copy(
            src_ref=to_z.at[0, 0], dst_ref=from_z.at[m], send_sem=z_send.at[m],
            recv_sem=z_recv.at[m], device_id=z_device(m, zh), device_id_type=MESH)

    def is_own(e):
        return jnp.logical_and(core == zh, e == (h * 4 + c) * 2 + core)

    def step_ring(layer):
        for way in range(2):
            around(layer, way).wait_recv()
            place = rem(p + 1 + 2 * way, 4)
            summed[layer, place, way] = (
                summed[layer, place, way].astype(F32) + half_way[layer, way].astype(F32)).astype(BF16)
            around(layer, 4 + way).start()

    def step_first(layer):
        for n in range(2, 6):
            around(layer, n).wait_recv()

        @pl.when(core == 0)
        def _():
            for half in range(2):
                for b in range(HALF // 128):
                    lanes = slice(b * 128, (b + 1) * 128)
                    total = (
                        summed[layer, p, half, :, lanes].astype(F32) + from_a[layer, 0, half, :, lanes].astype(F32)
                        + from_a[layer, 1, half, :, lanes].astype(F32))
                    total = jnp.concatenate([total, jnp.zeros((128 - PIECE, 128), F32)], axis=0)
                    first = half * HALF + b * 128
                    for row in range(first, first + 128, 64):
                        to_b[layer, row // 192, row % 192:row % 192 + 64, :] = total.T[row - first:row - first + 64].astype(BF16)

        @pl.when(core == 1)
        def _():
            for half in range(2):
                total = (
                    summed[layer, p, half].astype(F32) + from_a[layer, 0, half].astype(F32)
                    + from_a[layer, 1, half].astype(F32))
                for place in range(4):
                    value = total[:, place * PIECE:(place + 1) * PIECE]
                    value = jnp.concatenate([value, jnp.zeros((PIECE, 128 - PIECE), F32)], axis=1)
                    to_b[layer, place, half * PIECE:(half + 1) * PIECE, :] = value.astype(BF16)

        for i in range(1, 4):
            parcel(layer, i).start()

    def step_second():
        totals = []
        for layer in range(LAYERS):
            for i in range(1, 4):
                parcel(layer, i).wait_recv()
            total = to_b[layer, r].astype(F32)
            for i in range(3):
                total = total + from_b[layer, i].astype(F32)
            totals.append(total)
        for of_core in range(2):
            first = of_core * 48
            top = jnp.concatenate(
                [totals[2][:, first:first + 48], totals[1][:, first:first + 48], totals[0][:, first:first + 32]], axis=1)
            rest = totals[0][:, first + 32:first + 48].reshape(8, 3, 8, 16)
            rest = [rest[:, g].reshape(64, 16) for g in range(3)] + [jnp.zeros((64, 80), F32)]
            rest = jnp.concatenate(rest, axis=1)
            whole = jnp.concatenate([top.reshape(8, 24, 128), rest.reshape(8, 8, 128)], axis=1)
            to_z[of_core] = whole.astype(BF16)

        @pl.loop(0, 16)
        def _(e):
            @pl.when(is_own(e))
            def _():
                from_z[z] = to_z[core, h * 4 + c]

            @pl.when(jnp.logical_not(is_own(e)))
            def _():
                to_owner(e).start()

    def step_last():
        @pl.loop(0, 16)
        def _(m):
            @pl.when(jnp.logical_not(jnp.logical_and(core == zh, z == m)))
            def _():
                z_arrival(m).wait_recv()

        total = from_z[0].astype(F32)
        for m in range(1, 16):
            total = total + from_z[m].astype(F32)
        total = total * factor
        out_point[2] = total[0:24, 0:48]
        out_point[1] = total[0:24, 48:96]
        rest = jnp.concatenate([total[24:32, g * 16:(g + 1) * 16] for g in range(3)], axis=0)
        out_point[0] = jnp.concatenate([total[0:24, 96:128], rest], axis=1)

    tap_partners = (range(1, 8), range(1, 4), range(1, 16), range(1, 8))

    def tap_copy(step, i):
        place, peer = tap_peer(step, i)
        if step == 0:
            src, dst = taps_part.at[place], taps_in.at[0, i - 1]
        elif step == 3:
            src, dst = taps_one.at[2], taps_all.at[eighth]
        else:
            src, dst = taps_one.at[step - 1], taps_in.at[step, i - 1]
        return pltpu.make_async_remote_copy(
            src_ref=src, dst_ref=dst, send_sem=tap_send.at[step, i - 1], recv_sem=tap_recv.at[step, i - 1],
            device_id=peer, device_id_type=MESH)

    def tap_gathered(i):
        place = rem(eighth + 8 - i, 8)
        return pltpu.make_async_remote_copy(
            src_ref=taps_one.at[2], dst_ref=taps_all.at[place], send_sem=tap_send.at[3, i - 1],
            recv_sem=tap_recv.at[3, i - 1], device_id=tap_peer(3, i)[1], device_id_type=MESH)

    def tap_start(step):
        @pl.loop(tap_partners[step].start, tap_partners[step].stop)
        def _(i):
            tap_copy(step, i).start()

    def tap_step(step):
        @pl.loop(tap_partners[step].start, tap_partners[step].stop)
        def _(i):
            tap_copy(step, i).wait_recv()

        total = taps_part[eighth] if step == 0 else taps_one[step - 1]
        for i in tap_partners[step]:
            total = total + taps_in[step, i - 1]
        taps_one[step] = total
        if step == 2:
            taps_all[eighth] = total
        tap_start(step + 1)

    def tap_last():
        @pl.loop(1, 8)
        def _(i):
            tap_gathered(i).wait_recv()

        for layer in range(LAYERS):
            for t in range(3):
                for b in range(C // 128):
                    row = (layer * 3 + t) * (C // 128) + b
                    out_taps[layer, t:t + 1, b * 128:(b + 1) * 128] = taps_all[row // 7, row % 7:row % 7 + 1, :] * factor

    def send_back(a):
        @pl.loop(0, CHAIN - 1)
        def _(t):
            give_back(a, crossing_first(t)).start()

        own_out(a).start()

    send_cot(0)

    @pl.loop(0, PARTS * LAYERS)
    def _(n):
        a = div(n, LAYERS)
        layer = n - a * LAYERS

        @pl.when(layer == 0)
        def _():
            @pl.loop(1, CHAIN)
            def _(i):
                deal_tok(a, i, arriving=True).wait_recv()

            own_tok(a).wait()

        forward(a, layer)

    @pl.loop(0, PARTS * LAYERS)
    def _(n):
        a = div(n, LAYERS)
        layer = LAYERS - 1 - (n - a * LAYERS)

        @pl.when(layer == LAYERS - 1)
        def _():
            @pl.loop(1, CHAIN)
            def _(i):
                deal_cot(a, i, arriving=True).wait_recv()

            own_cot(a).wait()
            give_up(layer, a).start()

        backward(a, layer)

        @pl.when(layer > 0)
        def _():
            give_up(layer - 1, a).start()

        @pl.when(layer == 0)
        def _():
            send_back(a)

        @pl.when(a == PARTS - 1)
        def _():
            @pl.when(layer < LAYERS - 1)
            def _():
                step_ring(layer + 1)

            point_terms(layer)

    tap_terms()
    tap_start(0)

    @pl.loop(0, LAYERS)
    def _(n):
        @pl.when(n == 1)
        def _():
            step_ring(0)
            tap_step(0)

        @pl.when(n == 2)
        def _():
            tap_step(1)

        step_first(LAYERS - 1 - n)

    step_second()

    for a in range(PARTS):
        own_out(a).wait()

    @pl.loop(1, CHAIN)
    def _(i):
        for a in range(PARTS):
            give_back(a, i).wait_send()
        deal_tok(PARTS - 1, i).wait_send()
        deal_cot(PARTS - 1, i).wait_send()

    for i in (2, 4, 6, 7):
        deal_tok(0, i).wait_send()
        deal_cot(0, i).wait_send()

    @pl.loop(0, LAYERS)
    def _(layer):
        for a in range(PARTS):
            give_active(layer, a).wait_send()
            give_up(layer, a).wait_send()
        for n in range(6):
            around(layer, n).wait_send()
        for i in range(1, 4):
            parcel(layer, i).wait_send()
    for step in range(2):
        @pl.loop(tap_partners[step].start, tap_partners[step].stop)
        def _(i):
            tap_copy(step, i).wait_send()

    tap_step(2)
    for a in range(PARTS):
        @pl.loop(1, CHAIN)
        def _(i):
            given_back(a, i).wait_recv()

    @pl.loop(0, 16)
    def _(e):
        @pl.when(jnp.logical_not(is_own(e)))
        def _():
            to_owner(e).wait_send()

    @pl.loop(tap_partners[2].start, tap_partners[2].stop)
    def _(i):
        tap_copy(2, i).wait_send()

    step_last()
    tap_last()

    @pl.loop(tap_partners[3].start, tap_partners[3].stop)
    def _(i):
        tap_copy(3, i).wait_send()


def local(factor, tokens, cotangent, conv_kernel, point_weight):
    any_space = pl.BlockSpec(memory_space=pl.ANY)
    vmem = pl.BlockSpec(memory_space=pltpu.VMEM)
    part = (PARTS, CHAIN, ROWS, C)
    dealt = (CHAIN, PARTS, ROWS, C)
    scratch = [
        pltpu.VMEM(part, BF16),
        pltpu.VMEM((LAYERS, PARTS, CHAIN + 8, ROWS, C), BF16),
        pltpu.VMEM((LAYERS,) + part, F32),
        pltpu.VMEM((LAYERS, PARTS, CHAIN, ROWS, 128), F32),
        pltpu.VMEM((LAYERS,) + part, F32),
        pltpu.VMEM((LAYERS,) + part, BF16),
        pltpu.VMEM((LAYERS,) + part, BF16),
        pltpu.VMEM((CHAIN, ROWS, C), F32),
        pltpu.VMEM((CHAIN + 8, ROWS, C), BF16),
        pltpu.VMEM(part, BF16),
        pltpu.VMEM((LAYERS, C, C), BF16),
        pltpu.VMEM((LAYERS, 3, C), F32),
        pltpu.VMEM((LAYERS,) + part, BF16),
        pltpu.VMEM((LAYERS, PARTS, CHAIN, ROWS, HALF), BF16),
        pltpu.VMEM((LAYERS, 4, 2, PIECE, HALF), BF16),
        pltpu.VMEM((LAYERS, 2, PIECE, HALF), BF16),
        pltpu.VMEM((LAYERS, 2, 2, PIECE, HALF), BF16),
        pltpu.VMEM((LAYERS, 4, 192, 128), BF16),
        pltpu.VMEM((LAYERS, 3, 192, 128), BF16),
        pltpu.VMEM((2, 8, 32, 128), BF16),
        pltpu.VMEM((16, 32, 128), BF16),
        pltpu.VMEM((LAYERS, 3, 8, C), F32),
        pltpu.VMEM((8, 8, 128), F32),
        pltpu.VMEM((3, 8, 128), F32),
        pltpu.VMEM((3, 15, 8, 128), F32),
        pltpu.VMEM((8, 8, 128), F32),
        pltpu.SemaphoreType.DMA((PARTS, CHAIN - 1)),
        pltpu.SemaphoreType.DMA((PARTS, CHAIN - 1)),
        pltpu.SemaphoreType.DMA((PARTS, CHAIN - 1)),
        pltpu.SemaphoreType.DMA((PARTS, CHAIN - 1)),
        pltpu.SemaphoreType.DMA((PARTS, CHAIN - 1)),
        pltpu.SemaphoreType.DMA((PARTS, CHAIN - 1)),
        pltpu.SemaphoreType.DMA((3 * PARTS,)),
        pltpu.SemaphoreType.DMA((LAYERS + 1,)),
        pltpu.SemaphoreType.DMA((LAYERS, PARTS, 2)),
        pltpu.SemaphoreType.DMA((LAYERS, PARTS, 2)),
        pltpu.SemaphoreType.DMA((LAYERS, 6)),
        pltpu.SemaphoreType.DMA((LAYERS, 6)),
        pltpu.SemaphoreType.DMA((LAYERS, 3)),
        pltpu.SemaphoreType.DMA((LAYERS, 3)),
        pltpu.SemaphoreType.DMA((16,)),
        pltpu.SemaphoreType.DMA((16,)),
        pltpu.SemaphoreType.DMA((4, 15)),
        pltpu.SemaphoreType.DMA((4, 15)),
        pltpu.SemaphoreType.REGULAR((8, 2)),
        pltpu.SemaphoreType.REGULAR,
    ]
    out, out_point, out_taps = pl.pallas_call(
        functools.partial(kernel, factor),
        out_shape=(
            pltpu.VMEM((CHAIN, PARTS, ROWS, C), BF16),
            pltpu.VMEM((LAYERS, 24, 48), F32),
            pltpu.VMEM((LAYERS, 3, C), F32),
        ),
        in_specs=[any_space] * 4,
        out_specs=(any_space, vmem, vmem),
        scratch_shapes=scratch,
        compiler_params=pltpu.CompilerParams(collective_id=0, has_side_effects=True, vmem_limit_bytes=60 * 2**20),
        cost_estimate=pl.CostEstimate(flops=2 * 9 * SLAB * C * C, bytes_accessed=6 * 2**20, transcendentals=LAYERS * SLAB * C),
    )(tokens.reshape(dealt), cotangent.reshape(dealt), conv_kernel, point_weight)
    return out.reshape(tokens.shape), out_point, out_taps


def solution(mesh):
    factor = 1.0 / math.sqrt(mesh.shape["seq"] * mesh.shape["dp"] * SLAB)
    P = jax.sharding.PartitionSpec
    return jax.shard_map(
        functools.partial(local, factor),
        mesh=mesh,
        in_specs=(P("dp", "seq", None), P("dp", "seq", None), P(), P()),
        out_specs=(P("dp", "seq", None), P(None, "seq", "dp"), P()),
        check_vma=False,
    )
```

```python
import functools
import math

import jax
import jax.numpy as jnp
from jax import lax
from jax.experimental import pallas as pl
from jax.experimental.pallas import tpu as pltpu

EPSILON = 1e-06
MESH = pl.DeviceIdType.MESH
F32 = jnp.float32
BF16 = jnp.bfloat16

C = 768
LAYERS = 3
CHAIN = 8
ROWS = 16
PARTS = 2
SLAB = 256
COLS = 256
HALF = C // 2
PIECE = 96
GELU_A = math.sqrt(2.0 / math.pi)
GELU_B = 0.044715


def div(a, b):
    return lax.div(a, jnp.int32(b))


def rem(a, b):
    return lax.rem(a, jnp.int32(b))


def kernel(factor, tok, cot, taps_hbm, weight, out, out_point, out_taps, *scratch):
    (xin, normed, normal, inverse, slope, active, up, grad, grad_hid, w, taps, sib_active, sib_up, summed, half_way, from_a,
     to_b, from_b, to_z, from_z, taps_acc, taps_part, taps_one, taps_in, taps_all,
     tok_send, tok_recv, cot_send, cot_recv, out_send, out_recv, own_sem, w_sem, act_sem, up_sem, a_send, a_recv, red_send, red_recv,
     z_send, z_recv, tap_send, tap_recv, round_sem, pair_sem) = scratch
    seq = lax.axis_index("seq")
    dp = lax.axis_index("dp")
    k, c = div(seq, 4), rem(seq, 4)
    y, h = div(seq, 8), rem(k, 2)
    zh, core = div(dp, 8), rem(dp, 2)
    eighth = dp - zh * 8
    x = div(eighth, 2)
    block = zh * 2 + h
    p = x + core * (y - x)
    r = y + core * (x - y)

    def chain_peer(i):
        j = rem(k + i, CHAIN)
        return j, (j * 4 + c, dp)

    def first_peer(place):
        return seq + core * (place - y) * 8, dp + (1 - core) * (place - x) * 2

    def second_peer(i):
        place = rem(r + i, 4)
        return place, (seq + (1 - core) * (place - y) * 8, dp + core * (place - x) * 2)

    z = zh * 8 + h * 4 + c

    def z_device(place, of_core):
        half = div(place, 8)
        return y * 8 + place - half * 8, half * 8 + x * 2 + of_core

    def tap_peer(step, i):
        if step in (0, 3):
            place = rem(eighth + i, 8)
            return place, (seq, zh * 8 + place)
        if step == 1:
            place = rem(y + i, 4)
            return place, (place * 8 + h * 4 + c, dp)
        place = rem(z + i, 16)
        return place, z_device(place, core)

    barrier = pltpu.get_barrier_semaphore()

    def greet(peer):
        pl.semaphore_signal(barrier, inc=1, device_id=peer, device_id_type=MESH)

    @pl.loop(1, CHAIN)
    def _(i):
        greet(chain_peer(i)[1])
        greet(tap_peer(0, i)[1])

    above, below = z_device(rem(z + 1, 16), core), z_device(rem(z + 15, 16), core)
    greet(above)
    greet(below)

    def load(layer):
        return pltpu.make_async_copy(weight.at[layer], w.at[layer], w_sem.at[layer])

    load_taps = pltpu.make_async_copy(taps_hbm, taps, w_sem.at[LAYERS])
    load_taps.start()
    for layer in range(LAYERS):
        load(layer).start()

    pl.semaphore_wait(barrier, 16)

    def crossing_first(t):
        return 2 * t + 1 - 7 * div(t, 4)

    def deal_tok(a, i, arriving=False):
        j, peer = chain_peer(i)
        slot = rem(k + CHAIN - i, CHAIN) if arriving else k
        return pltpu.make_async_remote_copy(
            src_ref=tok.at[j, a], dst_ref=xin.at[a, slot], send_sem=tok_send.at[a, i - 1],
            recv_sem=tok_recv.at[a, i - 1], device_id=peer, device_id_type=MESH)

    def deal_cot(a, i, arriving=False):
        j, peer = chain_peer(i)
        slot = rem(k + CHAIN - i, CHAIN) if arriving else k
        return pltpu.make_async_remote_copy(
            src_ref=cot.at[j, a], dst_ref=up.at[LAYERS, a, slot], send_sem=cot_send.at[a, i - 1],
            recv_sem=cot_recv.at[a, i - 1], device_id=peer, device_id_type=MESH)

    def own_tok(a):
        return pltpu.make_async_copy(tok.at[k, a], xin.at[a, k], own_sem.at[2 * PARTS + a])

    def own_cot(a):
        return pltpu.make_async_copy(cot.at[k, a], up.at[LAYERS, a, k], own_sem.at[PARTS + a])

    def own_out(a):
        return pltpu.make_async_copy(up.at[0, a, k], out.at[k, a], own_sem.at[a])

    def give_back(a, i):
        j, peer = chain_peer(i)
        return pltpu.make_async_remote_copy(
            src_ref=up.at[0, a, j], dst_ref=out.at[k, a], send_sem=out_send.at[a, i - 1],
            recv_sem=out_recv.at[a, i - 1], device_id=peer, device_id_type=MESH)

    def given_back(a, i):
        j = rem(k + CHAIN - i, CHAIN)
        return pltpu.make_async_remote_copy(
            src_ref=up.at[0, a, j], dst_ref=out.at[j, a], send_sem=out_send.at[a, i - 1],
            recv_sem=out_recv.at[a, i - 1], device_id=chain_peer(i)[1], device_id_type=MESH)

    @pl.loop(0, PARTS)
    def _(a):
        @pl.loop(0, CHAIN - 1)
        def _(t):
            deal_tok(a, crossing_first(t)).start()

        own_tok(a).start()

    def send_cot(a):
        for i in (1, 3, 5):
            if a == 0:
                deal_tok(0, i).wait_send()
            else:
                deal_cot(0, i).wait_send()

        @pl.loop(0, CHAIN - 1)
        def _(t):
            deal_cot(a, crossing_first(t)).start()

        own_cot(a).start()

    def round_signal(t):
        pl.semaphore_signal(round_sem.at[t, 0], inc=1, device_id=above, device_id_type=MESH)
        pl.semaphore_signal(round_sem.at[t, 1], inc=1, device_id=below, device_id_type=MESH)

    def round_wait(t):
        pl.semaphore_wait(round_sem.at[t, 0], 1)
        pl.semaphore_wait(round_sem.at[t, 1], 1)

    @pl.loop(0, 3)
    def _(t):
        round_signal(t)
        round_wait(t)

    round_signal(3)

    def between_layers(n):
        @pl.when(n < 5)
        def _():
            round_wait(3 + n)

        @pl.when(n < 4)
        def _():
            round_signal(4 + n)

        @pl.when(n == 3)
        def _():
            send_cot(1)

        @pl.when(n == 4)
        def _():
            pl.semaphore_signal(pair_sem, inc=1, device_id=(seq, dp + 1 - 2 * core), device_id_type=MESH)

        @pl.when(n == 5)
        def _():
            pl.semaphore_wait(pair_sem, 1)

    zeros = jnp.zeros((4, ROWS, C), BF16)
    for layer in range(LAYERS):
        for a in range(PARTS):
            normed[layer, a, 0:4] = zeros
            normed[layer, a, 12:16] = zeros
    grad_hid[0:4] = zeros
    grad_hid[12:16] = zeros
    taps_acc[...] = jnp.zeros_like(taps_acc)
    taps_part[...] = jnp.zeros_like(taps_part)
    load_taps.wait()

    pair = (seq, dp + 1 - 2 * core)

    def give_active(layer, a):
        return pltpu.make_async_remote_copy(
            src_ref=active.at[layer, a], dst_ref=sib_active.at[layer, a], send_sem=act_sem.at[layer, a, 0],
            recv_sem=act_sem.at[layer, a, 1], device_id=pair, device_id_type=MESH)

    def give_up(layer, a):
        return pltpu.make_async_remote_copy(
            src_ref=up.at[layer + 1, a, :, :, pl.ds(pl.multiple_of((1 - core) * HALF, HALF), HALF)],
            dst_ref=sib_up.at[layer, a], send_sem=up_sem.at[layer, a, 0], recv_sem=up_sem.at[layer, a, 1],
            device_id=pair, device_id_type=MESH)

    def shift_of(layer):
        return 1 + layer + div(layer * (layer - 1), 2)

    def block_of_columns(n):
        return pl.ds(pl.multiple_of(n * COLS, COLS), COLS)

    def forward(a, layer):
        shift = shift_of(layer)

        @pl.loop(0, CHAIN, unroll=8)
        def _(j):
            value = xin[a, j].astype(F32)
            mean = jnp.sum(value * value, axis=-1, keepdims=True) * (1.0 / C)
            inv = lax.rsqrt(mean + EPSILON)
            value = value * inv
            inverse[layer, a, j] = jnp.broadcast_to(inv, (ROWS, 128))
            normal[layer, a, j] = value
            normed[layer, a, 4 + j] = value.astype(BF16)

        @pl.loop(0, CHAIN, unroll=8)
        def _(j):
            hid = (
                taps[layer, 0:1, :] * normed[layer, a, 4 + j - shift].astype(F32)
                + taps[layer, 1:2, :] * normed[layer, a, 4 + j].astype(F32)
                + taps[layer, 2:3, :] * normed[layer, a, 4 + j + shift].astype(F32)
            )
            square = hid * hid
            tanh = jnp.tanh(GELU_A * hid * (1.0 + GELU_B * square))
            half = 0.5 * (1.0 + tanh)
            active[layer, a, j] = (hid * half).astype(BF16)
            slope[layer, a, j] = half + (0.5 * GELU_A) * hid * (1.0 - tanh * tanh) * (1.0 + (3.0 * GELU_B) * square)

        give_active(layer, a).start()
        between_layers(a * LAYERS + layer)

        @pl.when(a == 0)
        def _():
            load(layer).wait()

        @pl.when(layer < LAYERS - 1)
        def _():
            @pl.loop(0, C // COLS)
            def _(n):
                cols = block_of_columns(n)
                product = jnp.dot(active[layer, a].reshape(CHAIN * ROWS, C), w[layer, :, cols], preferred_element_type=F32)
                xin[a, :, :, cols] = (
                    xin[a, :, :, cols].astype(F32) + product.reshape(CHAIN, ROWS, COLS)).astype(BF16)

    def backward(a, layer):
        shift = shift_of(layer)

        @pl.loop(0, C // COLS)
        def _(n):
            cols = block_of_columns(n)
            spread = lax.dot_general(
                up[layer + 1, a].reshape(CHAIN * ROWS, C), w[layer, cols, :], (((1,), (1,)), ((), ())),
                preferred_element_type=F32)
            grad_hid[4:12, :, cols] = (spread.reshape(CHAIN, ROWS, COLS) * slope[layer, a, :, :, cols]).astype(BF16)

        @pl.when(layer == LAYERS - 1)
        def _():
            grad[...] = up[layer + 1, a].astype(F32)

        @pl.loop(0, CHAIN, unroll=8)
        def _(j):
            mid = grad_hid[4 + j].astype(F32)
            for t in range(3):
                term = mid * normed[layer, a, 4 + j + (t - 1) * shift].astype(F32)
                taps_acc[layer, t] += term[0:8] + term[8:16]
            moved = (
                taps[layer, 1:2, :] * mid
                + taps[layer, 0:1, :] * grad_hid[4 + j + shift].astype(F32)
                + taps[layer, 2:3, :] * grad_hid[4 + j - shift].astype(F32)
            )
            value = normal[layer, a, j]
            mean = jnp.sum(moved * value, axis=-1, keepdims=True) * (1.0 / C)
            after = grad[j] + inverse[layer, a, j, :, 0:1] * (moved - value * mean)
            grad[j] = after
            up[layer, a, j] = after.astype(BF16)

    def point_terms(layer):
        for a in range(PARTS):
            give_active(layer, a).wait_recv()
            give_up(layer, a).wait_recv()
        mine = up[layer + 1, :, :, :, pl.ds(pl.multiple_of(core * HALF, HALF), HALF)].reshape(SLAB, HALF)
        rows = jnp.concatenate([mine, sib_up[layer].reshape(SLAB, HALF)], axis=0)
        over_rows = (((0,), (0,)), ((), ()))

        def acts(m):
            cols = slice(m * HALF, (m + 1) * HALF)
            return jnp.concatenate(
                [active[layer, :, :, :, cols].reshape(SLAB, HALF), sib_active[layer, :, :, :, cols].reshape(SLAB, HALF)],
                axis=0)

        @pl.when(core == 0)
        def _():
            for m in range(2):
                product = lax.dot_general(rows, acts(m), over_rows, preferred_element_type=F32)
                summed[layer, :, m] = product.astype(BF16).reshape(4, PIECE, HALF)

        @pl.when(core == 1)
        def _():
            for m in range(2):
                product = lax.dot_general(acts(m), rows, over_rows, preferred_element_type=F32)
                summed[layer, 2 * m:2 * m + 2] = product.astype(BF16).reshape(2, 2, PIECE, HALF)

        for n in range(4):
            around(layer, n).start()

    def tap_terms():
        for layer in range(LAYERS):
            for t in range(3):
                line = jnp.sum(taps_acc[layer, t], axis=0, keepdims=True)
                for b in range(C // 128):
                    row = (layer * 3 + t) * (C // 128) + b
                    taps_part[row // 7, row % 7:row % 7 + 1, :] = line[:, b * 128:(b + 1) * 128]

    def around(layer, n):
        way = n % 2
        place = rem(p + 1 + 2 * way, 4)
        if n < 2:
            src, dst = summed.at[layer, rem(p + 2, 4), way], half_way.at[layer, way]
        else:
            half = 1 - way if n < 4 else way
            src, dst = summed.at[layer, place, half], from_a.at[layer, way, half]
        return pltpu.make_async_remote_copy(
            src_ref=src, dst_ref=dst, send_sem=a_send.at[layer, n], recv_sem=a_recv.at[layer, n],
            device_id=first_peer(place), device_id_type=MESH)

    def parcel(layer, i):
        place, peer = second_peer(i)
        return pltpu.make_async_remote_copy(
            src_ref=to_b.at[layer, place], dst_ref=from_b.at[layer, i - 1], send_sem=red_send.at[layer, i - 1],
            recv_sem=red_recv.at[layer, i - 1], device_id=peer, device_id_type=MESH)

    def to_owner(e):
        place = div(e, 2)
        of_core = e - place * 2
        return pltpu.make_async_remote_copy(
            src_ref=to_z.at[of_core, place], dst_ref=from_z.at[z], send_sem=z_send.at[e],
            recv_sem=z_recv.at[z], device_id=z_device(core * 8 + place, of_core), device_id_type=MESH)

    def z_arrival(m):
        return pltpu.make_async_remote_copy(
            src_ref=to_z.at[0, 0], dst_ref=from_z.at[m], send_sem=z_send.at[m],
            recv_sem=z_recv.at[m], device_id=z_device(m, zh), device_id_type=MESH)

    def is_own(e):
        return jnp.logical_and(core == zh, e == (h * 4 + c) * 2 + core)

    def step_ring(layer):
        for way in range(2):
            around(layer, way).wait_recv()
            place = rem(p + 1 + 2 * way, 4)
            summed[layer, place, way] = (
                summed[layer, place, way].astype(F32) + half_way[layer, way].astype(F32)).astype(BF16)
            around(layer, 4 + way).start()

    def step_first(layer):
        for n in range(2, 6):
            around(layer, n).wait_recv()

        @pl.when(core == 0)
        def _():
            for half in range(2):
                for b in range(HALF // 128):
                    lanes = slice(b * 128, (b + 1) * 128)
                    total = (
                        summed[layer, p, half, :, lanes].astype(F32) + from_a[layer, 0, half, :, lanes].astype(F32)
                        + from_a[layer, 1, half, :, lanes].astype(F32))
                    total = jnp.concatenate([total, jnp.zeros((128 - PIECE, 128), F32)], axis=0)
                    first = half * HALF + b * 128
                    for row in range(first, first + 128, 64):
                        to_b[layer, row // 192, row % 192:row % 192 + 64, :] = total.T[row - first:row - first + 64].astype(BF16)

        @pl.when(core == 1)
        def _():
            for half in range(2):
                total = (
                    summed[layer, p, half].astype(F32) + from_a[layer, 0, half].astype(F32)
                    + from_a[layer, 1, half].astype(F32))
                for place in range(4):
                    value = total[:, place * PIECE:(place + 1) * PIECE]
                    value = jnp.concatenate([value, jnp.zeros((PIECE, 128 - PIECE), F32)], axis=1)
                    to_b[layer, place, half * PIECE:(half + 1) * PIECE, :] = value.astype(BF16)

        for i in range(1, 4):
            parcel(layer, i).start()

    def step_second():
        totals = []
        for layer in range(LAYERS):
            for i in range(1, 4):
                parcel(layer, i).wait_recv()
            total = to_b[layer, r].astype(F32)
            for i in range(3):
                total = total + from_b[layer, i].astype(F32)
            totals.append(total)
        for of_core in range(2):
            first = of_core * 48
            top = jnp.concatenate(
                [totals[2][:, first:first + 48], totals[1][:, first:first + 48], totals[0][:, first:first + 32]], axis=1)
            rest = totals[0][:, first + 32:first + 48].reshape(8, 3, 8, 16)
            rest = [rest[:, g].reshape(64, 16) for g in range(3)] + [jnp.zeros((64, 80), F32)]
            rest = jnp.concatenate(rest, axis=1)
            whole = jnp.concatenate([top.reshape(8, 24, 128), rest.reshape(8, 8, 128)], axis=1)
            to_z[of_core] = whole.astype(BF16)

        @pl.loop(0, 16)
        def _(e):
            @pl.when(is_own(e))
            def _():
                from_z[z] = to_z[core, h * 4 + c]

            @pl.when(jnp.logical_not(is_own(e)))
            def _():
                to_owner(e).start()

    def step_last():
        @pl.loop(0, 16)
        def _(m):
            @pl.when(jnp.logical_not(jnp.logical_and(core == zh, z == m)))
            def _():
                z_arrival(m).wait_recv()

        total = from_z[0].astype(F32)
        for m in range(1, 16):
            total = total + from_z[m].astype(F32)
        total = total * factor
        out_point[2] = total[0:24, 0:48]
        out_point[1] = total[0:24, 48:96]
        rest = jnp.concatenate([total[24:32, g * 16:(g + 1) * 16] for g in range(3)], axis=0)
        out_point[0] = jnp.concatenate([total[0:24, 96:128], rest], axis=1)

    tap_partners = (range(1, 8), range(1, 4), range(1, 16), range(1, 8))

    def tap_copy(step, i):
        place, peer = tap_peer(step, i)
        if step == 0:
            src, dst = taps_part.at[place], taps_in.at[0, i - 1]
        elif step == 3:
            src, dst = taps_one.at[2], taps_all.at[eighth]
        else:
            src, dst = taps_one.at[step - 1], taps_in.at[step, i - 1]
        return pltpu.make_async_remote_copy(
            src_ref=src, dst_ref=dst, send_sem=tap_send.at[step, i - 1], recv_sem=tap_recv.at[step, i - 1],
            device_id=peer, device_id_type=MESH)

    def tap_gathered(i):
        place = rem(eighth + 8 - i, 8)
        return pltpu.make_async_remote_copy(
            src_ref=taps_one.at[2], dst_ref=taps_all.at[place], send_sem=tap_send.at[3, i - 1],
            recv_sem=tap_recv.at[3, i - 1], device_id=tap_peer(3, i)[1], device_id_type=MESH)

    def tap_start(step):
        @pl.loop(tap_partners[step].start, tap_partners[step].stop)
        def _(i):
            tap_copy(step, i).start()

    def tap_step(step):
        @pl.loop(tap_partners[step].start, tap_partners[step].stop)
        def _(i):
            tap_copy(step, i).wait_recv()

        total = taps_part[eighth] if step == 0 else taps_one[step - 1]
        for i in tap_partners[step]:
            total = total + taps_in[step, i - 1]
        taps_one[step] = total
        if step == 2:
            taps_all[eighth] = total
        tap_start(step + 1)

    def tap_last():
        @pl.loop(1, 8)
        def _(i):
            tap_gathered(i).wait_recv()

        for layer in range(LAYERS):
            for t in range(3):
                for b in range(C // 128):
                    row = (layer * 3 + t) * (C // 128) + b
                    out_taps[layer, t:t + 1, b * 128:(b + 1) * 128] = taps_all[row // 7, row % 7:row % 7 + 1, :] * factor

    def send_back(a):
        @pl.loop(0, CHAIN - 1)
        def _(t):
            give_back(a, crossing_first(t)).start()

        own_out(a).start()

    send_cot(0)

    @pl.loop(0, PARTS * LAYERS)
    def _(n):
        a = div(n, LAYERS)
        layer = n - a * LAYERS

        @pl.when(layer == 0)
        def _():
            @pl.loop(1, CHAIN)
            def _(i):
                deal_tok(a, i, arriving=True).wait_recv()

            own_tok(a).wait()

        forward(a, layer)

    @pl.loop(0, PARTS * LAYERS)
    def _(n):
        a = div(n, LAYERS)
        layer = LAYERS - 1 - (n - a * LAYERS)

        @pl.when(layer == LAYERS - 1)
        def _():
            @pl.loop(1, CHAIN)
            def _(i):
                deal_cot(a, i, arriving=True).wait_recv()

            own_cot(a).wait()
            give_up(layer, a).start()

        backward(a, layer)

        @pl.when(layer > 0)
        def _():
            give_up(layer - 1, a).start()

        @pl.when(layer == 0)
        def _():
            send_back(a)

        @pl.when(a == PARTS - 1)
        def _():
            @pl.when(layer < LAYERS - 1)
            def _():
                step_ring(layer + 1)

            point_terms(layer)

    tap_terms()
    tap_start(0)

    @pl.loop(0, LAYERS)
    def _(n):
        @pl.when(n == 1)
        def _():
            step_ring(0)
            tap_step(0)

        @pl.when(n == 2)
        def _():
            tap_step(1)

        step_first(LAYERS - 1 - n)

    step_second()

    for a in range(PARTS):
        own_out(a).wait()

    @pl.loop(1, CHAIN)
    def _(i):
        for a in range(PARTS):
            give_back(a, i).wait_send()
        deal_tok(PARTS - 1, i).wait_send()
        deal_cot(PARTS - 1, i).wait_send()

    for i in (2, 4, 6, 7):
        deal_tok(0, i).wait_send()
        deal_cot(0, i).wait_send()

    @pl.loop(0, LAYERS)
    def _(layer):
        for a in range(PARTS):
            give_active(layer, a).wait_send()
            give_up(layer, a).wait_send()
        for n in range(6):
            around(layer, n).wait_send()
        for i in range(1, 4):
            parcel(layer, i).wait_send()
    for step in range(2):
        @pl.loop(tap_partners[step].start, tap_partners[step].stop)
        def _(i):
            tap_copy(step, i).wait_send()

    tap_step(2)
    for a in range(PARTS):
        @pl.loop(1, CHAIN)
        def _(i):
            given_back(a, i).wait_recv()

    @pl.loop(0, 16)
    def _(e):
        @pl.when(jnp.logical_not(is_own(e)))
        def _():
            to_owner(e).wait_send()

    @pl.loop(tap_partners[2].start, tap_partners[2].stop)
    def _(i):
        tap_copy(2, i).wait_send()

    step_last()
    tap_last()

    @pl.loop(tap_partners[3].start, tap_partners[3].stop)
    def _(i):
        tap_copy(3, i).wait_send()


def local(factor, tokens, cotangent, conv_kernel, point_weight):
    any_space = pl.BlockSpec(memory_space=pl.ANY)
    vmem = pl.BlockSpec(memory_space=pltpu.VMEM)
    part = (PARTS, CHAIN, ROWS, C)
    dealt = (CHAIN, PARTS, ROWS, C)
    scratch = [
        pltpu.VMEM(part, BF16),
        pltpu.VMEM((LAYERS, PARTS, CHAIN + 8, ROWS, C), BF16),
        pltpu.VMEM((LAYERS,) + part, F32),
        pltpu.VMEM((LAYERS, PARTS, CHAIN, ROWS, 128), F32),
        pltpu.VMEM((LAYERS,) + part, F32),
        pltpu.VMEM((LAYERS,) + part, BF16),
        pltpu.VMEM((LAYERS + 1,) + part, BF16),
        pltpu.VMEM((CHAIN, ROWS, C), F32),
        pltpu.VMEM((CHAIN + 8, ROWS, C), BF16),
        pltpu.VMEM((LAYERS, C, C), BF16),
        pltpu.VMEM((LAYERS, 3, C), F32),
        pltpu.VMEM((LAYERS,) + part, BF16),
        pltpu.VMEM((LAYERS, PARTS, CHAIN, ROWS, HALF), BF16),
        pltpu.VMEM((LAYERS, 4, 2, PIECE, HALF), BF16),
        pltpu.VMEM((LAYERS, 2, PIECE, HALF), BF16),
        pltpu.VMEM((LAYERS, 2, 2, PIECE, HALF), BF16),
        pltpu.VMEM((LAYERS, 4, 192, 128), BF16),
        pltpu.VMEM((LAYERS, 3, 192, 128), BF16),
        pltpu.VMEM((2, 8, 32, 128), BF16),
        pltpu.VMEM((16, 32, 128), BF16),
        pltpu.VMEM((LAYERS, 3, 8, C), F32),
        pltpu.VMEM((8, 8, 128), F32),
        pltpu.VMEM((3, 8, 128), F32),
        pltpu.VMEM((3, 15, 8, 128), F32),
        pltpu.VMEM((8, 8, 128), F32),
        pltpu.SemaphoreType.DMA((PARTS, CHAIN - 1)),
        pltpu.SemaphoreType.DMA((PARTS, CHAIN - 1)),
        pltpu.SemaphoreType.DMA((PARTS, CHAIN - 1)),
        pltpu.SemaphoreType.DMA((PARTS, CHAIN - 1)),
        pltpu.SemaphoreType.DMA((PARTS, CHAIN - 1)),
        pltpu.SemaphoreType.DMA((PARTS, CHAIN - 1)),
        pltpu.SemaphoreType.DMA((3 * PARTS,)),
        pltpu.SemaphoreType.DMA((LAYERS + 1,)),
        pltpu.SemaphoreType.DMA((LAYERS, PARTS, 2)),
        pltpu.SemaphoreType.DMA((LAYERS, PARTS, 2)),
        pltpu.SemaphoreType.DMA((LAYERS, 6)),
        pltpu.SemaphoreType.DMA((LAYERS, 6)),
        pltpu.SemaphoreType.DMA((LAYERS, 3)),
        pltpu.SemaphoreType.DMA((LAYERS, 3)),
        pltpu.SemaphoreType.DMA((16,)),
        pltpu.SemaphoreType.DMA((16,)),
        pltpu.SemaphoreType.DMA((4, 15)),
        pltpu.SemaphoreType.DMA((4, 15)),
        pltpu.SemaphoreType.REGULAR((8, 2)),
        pltpu.SemaphoreType.REGULAR,
    ]
    out, out_point, out_taps = pl.pallas_call(
        functools.partial(kernel, factor),
        out_shape=(
            pltpu.VMEM((CHAIN, PARTS, ROWS, C), BF16),
            pltpu.VMEM((LAYERS, 24, 48), F32),
            pltpu.VMEM((LAYERS, 3, C), F32),
        ),
        in_specs=[any_space] * 4,
        out_specs=(any_space, vmem, vmem),
        scratch_shapes=scratch,
        compiler_params=pltpu.CompilerParams(collective_id=0, has_side_effects=True, vmem_limit_bytes=60 * 2**20),
        cost_estimate=pl.CostEstimate(flops=2 * 9 * SLAB * C * C, bytes_accessed=6 * 2**20, transcendentals=LAYERS * SLAB * C),
    )(tokens.reshape(dealt), cotangent.reshape(dealt), conv_kernel, point_weight)
    return out.reshape(tokens.shape), out_point, out_taps


def solution(mesh):
    factor = 1.0 / math.sqrt(mesh.shape["seq"] * mesh.shape["dp"] * SLAB)
    P = jax.sharding.PartitionSpec
    return jax.shard_map(
        functools.partial(local, factor),
        mesh=mesh,
        in_specs=(P("dp", "seq", None), P("dp", "seq", None), P(), P()),
        out_specs=(P("dp", "seq", None), P(None, "seq", "dp"), P()),
        check_vma=False,
    )
```
